32 devices in a mesh: dp: 4 (over y, x), row: 2 (over core), col: 4 (over z).
Axes of the slice: x: 2, y: 2, z: 4, core: 2. Of those that a mesh axis runs over, the one named last changes fastest.
Arguments:
- block_input: bfloat16 [8192, 2048], P(('dp', 'col'), 'row'), may hold values from -6 to 6
- attn_gain: float32 [2048], P('row'), may hold values from 0.5 to 1.5
- attn_weight: bfloat16 [2048, 6144], P('row', 'col'), may hold values from -3.5 to 3.5
- out_weight: bfloat16 [2048, 2048], P('col', 'row'), may hold values from -1 to 1
- feed_gain: float32 [2048], P('row'), may hold values from 0.5 to 1.5
- gate_weight: bfloat16 [2048, 8192], P('row', 'col'), may hold values from -0.125 to 0.125
- up_weight: bfloat16 [2048, 8192], P('row', 'col'), may hold values from -0.125 to 0.125
- down_weight: bfloat16 [8192, 2048], P('col', 'row'), may hold values from -0.0625 to 0.0625
- out_cotangent: bfloat16 [8192, 2048], P(('dp', 'col'), 'row'), may hold values from -6 to 6
Outputs:
- block_output: bfloat16 [8192, 2048], P(('dp', 'col'), 'row')
- input_grad: float32 [8192, 2048], P(('dp', 'col'), 'row')
- attn_gain_grad: float32 [2048], P('row')
- attn_weight_grad: float32 [2048, 6144], P('row', 'col')
- out_weight_grad: float32 [2048, 2048], P('col', 'row')
- feed_gain_grad: float32 [2048], P('row')
- gate_weight_grad: float32 [2048, 8192], P('row', 'col')
- up_weight_grad: float32 [2048, 8192], P('row', 'col')
- down_weight_grad: float32 [8192, 2048], P('col', 'row')
The draws below stay inside these ranges and needn't reach their ends.
All inputs are finite; a program needn't handle non-finite values.
Results may differ from the reference program's by a relative error of at most 0.014.
Values may be sent and summed in bfloat16 or wider, within the bound.
No kernel may reach another device: no remote copies, remote signals or barrier semaphores. Data moves between devices by JAX's collectives and lax.ppermute only.
A program may use at most 320 MiB of HBM per device.

```python
import jax
import jax.numpy as jnp
from jax import lax

D = 2048
H = 32
HD = 64
FF = 8192
LEN = 1024
TOKENS = 8192


def draw_attn_weight(key, part):
    base = jnp.clip(jax.random.normal(key, (D, H, 3, HD), jnp.float32), -6.0, 6.0) * D ** (-0.5)
    return base.reshape(D, H * 3 * HD).astype(jnp.bfloat16)


def level_of(own_key, shape, cuts, least, high):
    gain = 1.0
    for axis_at, parts in cuts:
        steps = jax.random.uniform(jax.random.fold_in(jax.random.fold_in(own_key, 6), axis_at), (parts,), jnp.float32, least / len(cuts), high / len(cuts))
        gain = gain * jnp.repeat(jnp.exp(steps), shape[axis_at] // parts).reshape((-1,) + (1,) * (len(shape) - 1 - axis_at))
    return gain


def centred(rng, extent, deviation, reach, cuts=(), kind=jnp.bfloat16):
    entries = deviation * jax.random.normal(rng, extent, jnp.float32)
    if cuts:
        entries = entries * level_of(rng, extent, cuts, -0.22, 0.18)
    return jnp.clip(entries, -reach, reach).astype(kind)


def setup_inputs(seed: int = 0) -> dict:
    splits = jax.random.split(jax.random.key(seed), 10)
    return {
        "block_input": centred(splits[0], (TOKENS, D), 1.0, 6.0, ((0, 16), (1, 2))),
        "attn_gain": jnp.clip(1.0 + 0.1 * jax.random.normal(splits[1], (D,), jnp.float32), 0.5, 1.5),
        "attn_weight": draw_attn_weight(jax.random.fold_in(splits[9], 71), 0),
        "out_weight": centred(splits[3], (H * HD, D), (H * HD // 64) ** -0.5, 1.0, ((0, 4), (1, 2))),
        "feed_gain": jnp.clip(1.0 + 0.1 * jax.random.normal(splits[4], (D,), jnp.float32), 0.5, 1.5),
        "gate_weight": centred(splits[5], (D, FF), D ** -0.5, 0.125, ((0, 2), (1, 4))),
        "up_weight": centred(splits[6], (D, FF), D ** -0.5, 0.125, ((0, 2), (1, 4))),
        "down_weight": centred(splits[7], (FF, D), FF ** -0.5, 0.0625, ((0, 4), (1, 2))),
        "out_cotangent": centred(splits[8], (TOKENS, D), 1.0, 6.0, ((0, 16), (1, 2))),
    }


norm_epsilon = 1e-05
rope_base = 130000.0
masked_score = -1e+30

def rope_tables(positions):
    steps_half = jnp.arange(HD // 2).astype(jnp.float32)
    frequency = rope_base ** (-2.0 * steps_half / HD)
    angles = positions.astype(jnp.float32)[:, None] * frequency[None, :]
    return (jnp.cos(angles)[:, None, :], jnp.sin(angles)[:, None, :])

def rotate(tensor, cosines, sines, sign):
    half = tensor.shape[-1] // 2
    first = tensor[..., :half]
    second = tensor[..., half:]
    return jnp.concatenate([first * cosines - second * (sign * sines), second * cosines + first * (sign * sines)], axis=-1)

def transposed_left(left, right):
    return lax.dot_general(left, right, (((0,), (0,)), ((), ())), preferred_element_type=jnp.float32)

def transposed_right(left, right):
    return lax.dot_general(left, right, (((1,), (1,)), ((), ())), preferred_element_type=jnp.float32)

def heads_first(tensor):
    return jnp.transpose(tensor, (1, 0, 2))

def causal_scores(query, key_mat):
    allowed = jnp.arange(LEN)[:, None] >= jnp.arange(LEN)[None, :]
    scores = transposed_right(query, key_mat) * HD ** (-0.5)
    return jnp.where(allowed, scores, masked_score)

def head_forward(operands):
    query, key_mat, value = operands
    scores = causal_scores(query, key_mat)
    peak = lax.optimization_barrier(jnp.max(scores, axis=1, keepdims=True))
    log_total = peak + jnp.log(lax.optimization_barrier(jnp.sum(jnp.exp(scores - peak), axis=1, keepdims=True)))
    probs = jnp.exp(scores - log_total).astype(jnp.bfloat16)
    return (jnp.dot(probs, value, preferred_element_type=jnp.float32).astype(jnp.bfloat16), log_total[:, 0])

def head_backward(operands):
    query, key_mat, value, log_total, grad_out = operands
    scores = causal_scores(query, key_mat)
    back_probs = jnp.exp(scores - log_total[:, None])
    value_grad = transposed_left(back_probs.astype(jnp.bfloat16), grad_out)
    prob_grad = transposed_right(grad_out, value)
    center = lax.optimization_barrier(jnp.sum(back_probs * prob_grad, axis=1, keepdims=True))
    score_grad = (back_probs * (prob_grad - center) * HD ** (-0.5)).astype(jnp.bfloat16)
    query_grad = jnp.dot(score_grad, key_mat, preferred_element_type=jnp.float32)
    key_grad = transposed_left(score_grad, query)
    return (query_grad, key_grad, value_grad)

def reference(block_input, attn_gain, attn_weight, out_weight, feed_gain, gate_weight, up_weight, down_weight, out_cotangent):

    def sequence_step(carry, batch):
        seq_input, seq_cotangent = batch
        inputs = seq_input.astype(jnp.float32)
        first_scale = lax.rsqrt(lax.optimization_barrier(jnp.mean(inputs * inputs, axis=1, keepdims=True)) + norm_epsilon)
        first_normed = (inputs * first_scale * attn_gain).astype(jnp.bfloat16)
        projected = jnp.dot(first_normed, attn_weight, preferred_element_type=jnp.float32).reshape(LEN, H, 3, HD)
        cosines, sines = rope_tables(jnp.arange(LEN))
        queries = rotate(projected[:, :, 0], cosines, sines, 1.0).astype(jnp.bfloat16)
        keys = rotate(projected[:, :, 1], cosines, sines, 1.0).astype(jnp.bfloat16)
        values = projected[:, :, 2].astype(jnp.bfloat16)
        head_out, log_totals = lax.map(head_forward, (heads_first(queries), heads_first(keys), heads_first(values)))
        attended = heads_first(head_out).reshape(LEN, H * HD)
        residual = inputs + jnp.dot(attended, out_weight, preferred_element_type=jnp.float32)
        second_scale = lax.rsqrt(lax.optimization_barrier(jnp.mean(residual * residual, axis=1, keepdims=True)) + norm_epsilon)
        second_normed = (residual * second_scale * feed_gain).astype(jnp.bfloat16)
        gate = jnp.dot(second_normed, gate_weight, preferred_element_type=jnp.float32)
        upper = jnp.dot(second_normed, up_weight, preferred_element_type=jnp.float32)
        hidden = (jax.nn.silu(gate) * upper).astype(jnp.bfloat16)
        output = (residual + jnp.dot(hidden, down_weight, preferred_element_type=jnp.float32)).astype(jnp.bfloat16)
        cotangent = seq_cotangent.astype(jnp.float32)
        down_grad = transposed_left(hidden, seq_cotangent)
        hidden_grad = transposed_right(seq_cotangent, down_weight)
        gate_sigmoid = jax.nn.sigmoid(gate)
        gate_grad = (hidden_grad * upper * gate_sigmoid * (1.0 + gate * (1.0 - gate_sigmoid))).astype(jnp.bfloat16)
        upper_grad = (hidden_grad * jax.nn.silu(gate)).astype(jnp.bfloat16)
        gate_w_grad = transposed_left(second_normed, gate_grad)
        up_w_grad = transposed_left(second_normed, upper_grad)
        second_grad = transposed_right(gate_grad, gate_weight) + transposed_right(upper_grad, up_weight)
        second_hat = residual * second_scale
        feed_part = lax.optimization_barrier(jnp.sum(second_grad * second_hat, axis=0))
        weighted = second_grad * feed_gain
        residual_grad = cotangent + second_scale * (weighted - second_hat * lax.optimization_barrier(jnp.mean(weighted * second_hat, axis=1, keepdims=True)))
        residual_low = residual_grad.astype(jnp.bfloat16)
        out_w_grad = transposed_left(attended, residual_low)
        attended_grad = transposed_right(residual_low, out_weight).astype(jnp.bfloat16).reshape(LEN, H, HD)
        query_grad, key_grad, value_grad = lax.map(head_backward, (heads_first(queries), heads_first(keys), heads_first(values), log_totals, heads_first(attended_grad)))
        query_pre = rotate(heads_first(query_grad), cosines, sines, -1.0)
        key_pre = rotate(heads_first(key_grad), cosines, sines, -1.0)
        projected_grad = jnp.stack([query_pre, key_pre, heads_first(value_grad)], axis=2).reshape(LEN, H * 3 * HD).astype(jnp.bfloat16)
        attn_w_grad = transposed_left(first_normed, projected_grad)
        first_grad = transposed_right(projected_grad, attn_weight)
        first_hat = inputs * first_scale
        attn_part = lax.optimization_barrier(jnp.sum(first_grad * first_hat, axis=0))
        weighted_first = first_grad * attn_gain
        input_rows = residual_grad + first_scale * (weighted_first - first_hat * lax.optimization_barrier(jnp.mean(weighted_first * first_hat, axis=1, keepdims=True)))
        updates = (attn_part, attn_w_grad, out_w_grad, feed_part, gate_w_grad, up_w_grad, down_grad)
        carry = tuple((total + extra for total, extra in zip(carry, updates)))
        return (carry, (output, input_rows))
    seq_total = block_input.shape[0] // LEN
    width = block_input.shape[1]
    start_carry = (jnp.zeros((width,), jnp.float32), jnp.zeros(attn_weight.shape, jnp.float32), jnp.zeros(out_weight.shape, jnp.float32), jnp.zeros((width,), jnp.float32), jnp.zeros(gate_weight.shape, jnp.float32), jnp.zeros(up_weight.shape, jnp.float32), jnp.zeros(down_weight.shape, jnp.float32))
    sums, (outputs, input_rows) = lax.scan(sequence_step, start_carry, (block_input.reshape(seq_total, LEN, width), out_cotangent.reshape(seq_total, LEN, width)))
    return (outputs.reshape(seq_total * LEN, width), input_rows.reshape(seq_total * LEN, width), sums[0], sums[1], sums[2], sums[3], sums[4], sums[5], sums[6])
```

```python
import functools

import jax
import jax.numpy as jnp
from jax import lax
from jax.experimental import pallas as pl
from jax.experimental.pallas import tpu as pltpu
from jax.sharding import PartitionSpec as P

HD = 64
LEN = 1024
PAIR = 6 * HD
BLOCK = 256

norm_epsilon = 1e-05
rope_base = 130000.0
masked_score = -1e30
LOG2E = 1.4426950408889634
BF = jnp.bfloat16
F32 = jnp.float32
MIB = 1024 * 1024


def nn(left, right):
    return lax.dot_general(left, right, (((1,), (0,)), ((), ())), preferred_element_type=F32)


def nt(left, right):
    return lax.dot_general(left, right, (((1,), (1,)), ((), ())), preferred_element_type=F32)


def tn(left, right):
    return lax.dot_general(left, right, (((0,), (0,)), ((), ())), preferred_element_type=F32)


def params(mib):
    return pltpu.CompilerParams(vmem_limit_bytes=mib * MIB)


def rope_tables():
    steps_half = jnp.arange(HD // 2).astype(F32)
    frequency = rope_base ** (-2.0 * steps_half / HD)
    angles = jnp.arange(LEN).astype(F32)[:, None] * frequency[None, :]
    cos, sin = jnp.cos(angles), jnp.sin(angles)
    return (
        jnp.concatenate([cos] * 4, axis=1),
        jnp.concatenate([-sin, sin] * 2, axis=1),
    )


def project_kernel(xo, xt, go, gt, wo, wt, cos, sin, no, nt_, out):
    @pl.when(pl.program_id(0) == 0)
    def _():
        rows = 256
        for i in range(LEN // rows):
            at = slice(i * rows, (i + 1) * rows)
            a = xo[at, :].astype(F32)
            b = xt[at, :].astype(F32)
            total = jnp.sum(a * a, axis=1, keepdims=True) + jnp.sum(b * b, axis=1, keepdims=True)
            scale = lax.rsqrt(total / (a.shape[1] + b.shape[1]) + norm_epsilon)
            no[at, :] = (a * scale * go[...]).astype(BF)
            nt_[at, :] = (b * scale * gt[...]).astype(BF)

    proj = nn(no[...], wo[...]) + nn(nt_[...], wt[...])
    lane = lax.broadcasted_iota(jnp.int32, (LEN, 128), 1)
    low = (lane % HD) < HD // 2
    for piece in range(3):
        part = proj[:, piece * 128 : (piece + 1) * 128]
        swapped = jnp.where(low, pltpu.roll(part, 96, 1), pltpu.roll(part, 32, 1))
        turned = part * cos[...] + swapped * sin[...]
        if piece == 1:
            turned = jnp.where(lane < HD, part, turned)
        if piece == 2:
            turned = jnp.where(lane < HD, turned, part)
        out[:, piece * 128 : (piece + 1) * 128] = turned.astype(BF)


def project(xo, xt, go, gt, wo, wt, cos, sin):
    half, columns = wo.shape
    fixed = lambda shape: pl.BlockSpec(shape, lambda i: (0, 0))
    weight = pl.BlockSpec((half, PAIR), lambda i: (0, i))
    return pl.pallas_call(
        project_kernel,
        grid=(columns // PAIR,),
        in_specs=[fixed((LEN, half))] * 2
        + [fixed((1, half))] * 2
        + [weight] * 2
        + [fixed((LEN, 128))] * 2,
        out_specs=[fixed((LEN, half))] * 2 + [pl.BlockSpec((LEN, PAIR), lambda i: (0, i))],
        out_shape=[jax.ShapeDtypeStruct((LEN, half), BF)] * 2
        + [jax.ShapeDtypeStruct((LEN, columns), BF)],
        compiler_params=params(56),
        cost_estimate=pl.CostEstimate(
            flops=4 * LEN * half * columns, bytes_accessed=2 * LEN * half * 8, transcendentals=0
        ),
    )(xo, xt, go, gt, wo, wt, cos, sin)


def head_parts(qkv, head):
    at = head * 3 * HD
    return qkv[:, at : at + HD], qkv[:, at + HD : at + 2 * HD], qkv[:, at + 2 * HD : at + 3 * HD]


def attend_kernel(qkv, out, log_total):
    scale = HD**-0.5 * LOG2E
    row = lax.broadcasted_iota(jnp.int32, (BLOCK, BLOCK), 0)
    col = lax.broadcasted_iota(jnp.int32, (BLOCK, BLOCK), 1)
    for head in range(2):
        q, k, v = head_parts(qkv, head)
        for i in range(LEN // BLOCK):
            start, end = i * BLOCK, (i + 1) * BLOCK
            scores = nt(q[start:end], k[:end])
            last = jnp.where(row >= col, scores[:, start:], masked_score)
            scores = jnp.concatenate([scores[:, :start], last], axis=1) if i else last
            peak = jnp.max(scores, axis=1, keepdims=True)
            probs = jnp.exp2((scores - peak) * scale)
            total = jnp.sum(probs, axis=1, keepdims=True)
            mixed = nn(probs.astype(BF), v[:end]) / total
            out[start:end, head * HD : (head + 1) * HD] = mixed.astype(BF)
            log_total[start:end, head * HD : (head + 1) * HD] = jnp.broadcast_to(
                peak * scale + jnp.log2(total), (BLOCK, HD)
            )


def attend(qkv):
    pairs = qkv.shape[1] // PAIR
    narrow = pl.BlockSpec((LEN, 2 * HD), lambda i: (0, i))
    return pl.pallas_call(
        attend_kernel,
        grid=(pairs,),
        in_specs=[pl.BlockSpec((LEN, PAIR), lambda i: (0, i))],
        out_specs=[narrow, narrow],
        out_shape=[
            jax.ShapeDtypeStruct((LEN, pairs * 2 * HD), BF),
            jax.ShapeDtypeStruct((LEN, pairs * 2 * HD), F32),
        ],
        compiler_params=params(48),
        cost_estimate=pl.CostEstimate(
            flops=pairs * 8 * LEN * LEN * 256, bytes_accessed=LEN * pairs * 1500, transcendentals=0
        ),
    )(qkv)


def attend_back_kernel(qkv, grad, mixed, log_total, cos, sin, out):
    scale = HD**-0.5 * LOG2E
    row = lax.broadcasted_iota(jnp.int32, (BLOCK, BLOCK), 0)
    col = lax.broadcasted_iota(jnp.int32, (BLOCK, BLOCK), 1)
    blocks = LEN // BLOCK
    totals = jnp.transpose(log_total[...])
    product = jnp.transpose(grad[...].astype(F32) * mixed[...].astype(F32))
    cosines, sines = cos[:, :HD], sin[:, :HD]

    def unturn(part, start, end):
        swapped = jnp.concatenate([part[:, HD // 2 :], part[:, : HD // 2]], axis=1)
        return (part * cosines[start:end] - swapped * sines[start:end]).astype(BF)

    for head in range(2):
        q, k, v = head_parts(qkv, head)
        at = head * 3 * HD
        g = grad[:, head * HD : (head + 1) * HD]
        total = totals[head * HD : head * HD + 1]
        center = jnp.sum(product[head * HD : (head + 1) * HD], axis=0, keepdims=True)
        query_grad = [None] * blocks
        for j in range(blocks):
            start, end = j * BLOCK, (j + 1) * BLOCK
            scores = nt(k[start:end], q[start:])
            probs = jnp.exp2(scores * scale - total[:, start:])
            first = jnp.where(col >= row, probs[:, :BLOCK], 0.0)
            probs = jnp.concatenate([first, probs[:, BLOCK:]], axis=1) if end < LEN else first
            out[start:end, at + 2 * HD : at + 3 * HD] = nn(probs.astype(BF), g[start:]).astype(BF)
            prob_grad = nt(v[start:end], g[start:])
            score_grad = (probs * (prob_grad - center[:, start:])).astype(BF)
            key_grad = nn(score_grad, q[start:]) * (HD**-0.5)
            out[start:end, at + HD : at + 2 * HD] = unturn(key_grad, start, end)
            term = tn(k[start:end], score_grad)
            for b in range(j, blocks):
                here = term[:, (b - j) * BLOCK : (b - j + 1) * BLOCK]
                query_grad[b] = here if query_grad[b] is None else query_grad[b] + here
        for b in range(blocks):
            start, end = b * BLOCK, (b + 1) * BLOCK
            out[start:end, at : at + HD] = unturn(
                jnp.transpose(query_grad[b]) * (HD**-0.5), start, end
            )


def attend_back(qkv, grad, mixed, log_total, cos, sin):
    pairs = qkv.shape[1] // PAIR
    wide = pl.BlockSpec((LEN, PAIR), lambda i: (0, i))
    narrow = pl.BlockSpec((LEN, 2 * HD), lambda i: (0, i))
    fixed = pl.BlockSpec((LEN, 128), lambda i: (0, 0))
    return pl.pallas_call(
        attend_back_kernel,
        grid=(pairs,),
        in_specs=[wide, narrow, narrow, narrow, fixed, fixed],
        out_specs=wide,
        out_shape=jax.ShapeDtypeStruct((LEN, pairs * PAIR), BF),
        compiler_params=params(56),
        cost_estimate=pl.CostEstimate(
            flops=pairs * 12 * LEN * LEN * 256, bytes_accessed=LEN * pairs * 2500, transcendentals=0
        ),
    )(qkv, grad, mixed, log_total, cos, sin)


def residual_kernel(count, *refs):
    mixed = refs[:count]
    wo, wt, xo, xt, go, gt, ro, rt, no, nt_ = refs[count:]
    a = xo[...].astype(F32)
    b = xt[...].astype(F32)
    for step in range(count):
        left = mixed[step][...]
        a = a + nn(left, wo[step])
        b = b + nn(left, wt[step])
    total = jnp.sum(a * a, axis=1, keepdims=True) + jnp.sum(b * b, axis=1, keepdims=True)
    scale = lax.rsqrt(total / (a.shape[1] + b.shape[1]) + norm_epsilon)
    ro[...] = a
    rt[...] = b
    no[...] = (a * scale * go[...]).astype(BF)
    nt_[...] = (b * scale * gt[...]).astype(BF)


def add_residual(mixed, wo, wt, xo, xt, go, gt):
    count, depth, half = wo.shape
    rows = 256
    left = pl.BlockSpec((rows, depth), lambda i: (i, 0))
    weight = pl.BlockSpec((count, depth, half), lambda i: (0, 0, 0))
    part = pl.BlockSpec((rows, half), lambda i: (i, 0))
    gain = pl.BlockSpec((1, half), lambda i: (0, 0))
    return pl.pallas_call(
        functools.partial(residual_kernel, count),
        grid=(LEN // rows,),
        in_specs=[left] * count + [weight] * 2 + [part] * 2 + [gain] * 2,
        out_specs=[part] * 4,
        out_shape=[jax.ShapeDtypeStruct((LEN, half), F32)] * 2
        + [jax.ShapeDtypeStruct((LEN, half), BF)] * 2,
        compiler_params=params(56),
        cost_estimate=pl.CostEstimate(
            flops=4 * LEN * half * count * depth, bytes_accessed=LEN * half * 20, transcendentals=0
        ),
    )(*mixed, wo, wt, xo, xt, go, gt)


def feed_kernel(no, nt_, co, ct, gwo, gwt, uwo, uwt, dwo, dwt, hidden, gate_grad, upper_grad):
    gate = nn(no[...], gwo[...]) + nn(nt_[...], gwt[...])
    upper = nn(no[...], uwo[...]) + nn(nt_[...], uwt[...])
    sigmoid = 1.0 / (1.0 + jnp.exp(-gate))
    silu = gate * sigmoid
    hidden[...] = (silu * upper).astype(BF)
    hidden_grad = nt(co[...], dwo[...]) + nt(ct[...], dwt[...])
    gate_grad[...] = (hidden_grad * upper * sigmoid * (1.0 + gate * (1.0 - sigmoid))).astype(BF)
    upper_grad[...] = (hidden_grad * silu).astype(BF)


def feed(no, nt_, co, ct, gwo, gwt, uwo, uwt, dwo, dwt):
    half, units = gwo.shape
    tokens = pl.BlockSpec((LEN, half), lambda i: (0, 0))
    weight = pl.BlockSpec((half, BLOCK), lambda i: (0, i))
    down = pl.BlockSpec((BLOCK, half), lambda i: (i, 0))
    out = pl.BlockSpec((LEN, BLOCK), lambda i: (0, i))
    return pl.pallas_call(
        feed_kernel,
        grid=(units // BLOCK,),
        in_specs=[tokens] * 4 + [weight] * 4 + [down] * 2,
        out_specs=[out] * 3,
        out_shape=[jax.ShapeDtypeStruct((LEN, units), BF)] * 3,
        compiler_params=params(60),
        cost_estimate=pl.CostEstimate(
            flops=12 * LEN * half * units, bytes_accessed=12 * half * units, transcendentals=0
        ),
    )(no, nt_, co, ct, gwo, gwt, uwo, uwt, dwo, dwt)


def swap_row(values):
    return lax.ppermute(values, "row", [(0, 1), (1, 0)])


class Ring:
    def __init__(self):
        count = lax.axis_size("col")
        order = list(range(0, count, 2)) + list(range(count - 1 - count % 2, 0, -2))
        self.count = count
        self.order = order
        self.table = jnp.array(order, jnp.int32)
        place = [order.index(i) for i in range(count)]
        self.here = jnp.array(place, jnp.int32)[lax.axis_index("col")]
        self.core = lax.axis_index("row")

    def shift(self, values, by):
        count, order = self.count, self.order
        pairs = [(order[p], order[(p + by) % count]) for p in range(count)]
        return lax.ppermute(values, "col", pairs)

    def owner(self, back):
        return self.table[(self.here - back) % self.count]

    def split(self, owner):
        per = self.count // 2
        return owner // per, owner % per

    def gather_list(self, values):
        out = [values]
        for _ in range(self.count - 1):
            out.append(self.shift(out[-1], 1))
        return out

    def place(self, blocks, direction):
        rows, columns = blocks[0].shape
        out = jnp.zeros((self.count * rows, columns), blocks[0].dtype)
        for step, block in enumerate(blocks):
            sequence, at = self.split(self.owner(direction * step))
            slot = jnp.where(sequence == self.core, 0, self.count // 2) + at
            out = lax.dynamic_update_slice(out, block, (slot * rows, 0))
        return out

    def gather_tokens(self, values):
        both = self.place(self.gather_list(values), 1)
        half = both.shape[0] // 2
        return both[:half], swap_row(both[half:])

    def reduce_tokens(self, own, other):
        other = swap_row(other.astype(BF))
        own = own.astype(BF)
        rows = own.shape[0] * 2 // self.count

        def term(back):
            sequence, at = self.split(self.owner(back))
            take = lambda values: lax.dynamic_slice_in_dim(values, at * rows, rows, 0)
            return jnp.where(sequence == self.core, take(own), take(other))

        total = term(1)
        for step in range(1, self.count):
            total = self.shift(total.astype(BF), 1).astype(F32) + term(step + 1).astype(F32)
        return total


def reduce_weights(own, other):
    mine = own
    theirs = swap_row(other)
    rows = own.shape[0]
    index = lax.axis_index("dp")
    bit_x, bit_y = index % 2, index // 2
    hop_x = lambda v: lax.ppermute(v, "dp", [(i, i ^ 1) for i in range(4)])
    hop_y = lambda v: lax.ppermute(v, "dp", [(i, i ^ 2) for i in range(4)])

    def first(base, bit):
        at = base + bit * (rows // 4)
        take = lambda v: lax.dynamic_slice_in_dim(v, at, rows // 4, 0).astype(F32)
        return take(mine) + take(theirs)

    def part(values, bit):
        size = values.shape[0] // 2
        return lax.dynamic_slice_in_dim(values, bit * size, size, 0)

    pieces = []
    for base, bit_1, hop_1, bit_2, hop_2 in (
        (0, bit_x, hop_x, bit_y, hop_y),
        (rows // 2, bit_y, hop_y, bit_x, hop_x),
    ):
        got = hop_1(first(base, 1 - bit_1).astype(BF))
        kept = first(base, bit_1) + got.astype(F32)
        got = hop_2(part(kept, 1 - bit_2).astype(BF))
        kept = (part(kept, bit_2) + got.astype(F32)).astype(BF)
        got = hop_2(kept)
        low = jnp.where(bit_2 == 0, kept, got)
        high = jnp.where(bit_2 == 0, got, kept)
        both = jnp.concatenate([low, high], axis=0)
        got = hop_1(both)
        pieces.append(jnp.where(bit_1 == 0, both, got))
        pieces.append(jnp.where(bit_1 == 0, got, both))
    return jnp.concatenate(pieces, axis=0).astype(F32)


def gather_out_weight(ring, weight):
    rows, half = weight.shape
    size = rows // 4
    index = lax.axis_index("dp")
    quarter = lax.dynamic_slice_in_dim(weight, index * size, size, 0)
    held = jnp.stack(ring.gather_list(quarter), axis=0)
    hop_x = lambda v: lax.ppermute(v, "dp", [(i, i ^ 1) for i in range(4)])
    hop_y = lambda v: lax.ppermute(v, "dp", [(i, i ^ 2) for i in range(4)])
    beside = hop_x(held)
    even = index % 2 == 0
    pair = jnp.concatenate(
        [jnp.where(even, held, beside), jnp.where(even, beside, held)], axis=1
    )
    beside = hop_y(pair)
    low = index // 2 == 0
    own = jnp.concatenate([jnp.where(low, pair, beside), jnp.where(low, beside, pair)], axis=1)
    return own, swap_row(own)


def row_total(values):
    return values + swap_row(values)


def shards(
    block_input,
    attn_gain,
    attn_weight,
    out_weight,
    feed_gain,
    gate_weight,
    up_weight,
    down_weight,
    out_cotangent,
):
    ring = Ring()
    rows, half = block_input.shape
    width = 2 * half
    cos, sin = rope_tables()
    go1, go2 = attn_gain[None, :], feed_gain[None, :]
    gains = swap_row(jnp.concatenate([go1, go2], axis=0))
    gt1, gt2 = gains[:1], gains[1:]

    xo, xt = ring.gather_tokens(block_input)
    aw_other = swap_row(attn_weight)
    n1o, n1t, qkv = project(xo, xt, go1, gt1, attn_weight, aw_other, cos, sin)
    mixed, log_total = attend(qkv)
    ow_own, ow_other = gather_out_weight(ring, out_weight)
    co, ct = ring.gather_tokens(out_cotangent)
    mixed_all = ring.gather_list(mixed)
    res_o, res_t, n2o, n2t = add_residual(mixed_all, ow_own, ow_other, xo, xt, go2, gt2)

    gw_other, uw_other, dw_other = swap_row(gate_weight), swap_row(up_weight), swap_row(down_weight)
    hidden, gate_grad, upper_grad = feed(
        n2o, n2t, co, ct, gate_weight, gw_other, up_weight, uw_other, down_weight, dw_other
    )
    second_grad = ring.reduce_tokens(
        nt(gate_grad, gate_weight) + nt(upper_grad, up_weight),
        nt(gate_grad, gw_other) + nt(upper_grad, uw_other),
    )

    sequence, at = ring.split(lax.axis_index("col"))
    take = lambda v: lax.dynamic_slice_in_dim(v, at * rows, rows, 0)
    residual = jnp.where(sequence == ring.core, take(res_o), swap_row(take(res_t)))
    second_scale = lax.rsqrt(
        row_total(jnp.sum(residual * residual, axis=1, keepdims=True)) / width + norm_epsilon
    )
    second_hat = residual * second_scale
    feed_part = jnp.sum(second_grad * second_hat, axis=0)
    weighted = second_grad * go2
    second_mean = row_total(jnp.sum(weighted * second_hat, axis=1, keepdims=True)) / width
    residual_grad = out_cotangent.astype(F32) + second_scale * (weighted - second_hat * second_mean)
    residual_low = residual_grad.astype(BF)

    size = rows // 2
    mine = lax.dynamic_slice_in_dim(residual_low, ring.core * size, size, 0)
    theirs = swap_row(lax.dynamic_slice_in_dim(residual_low, (1 - ring.core) * size, size, 0))
    heads = mixed.shape[1]
    grads = (
        nt(mine, ow_own.reshape(-1, half)) + nt(theirs, ow_other.reshape(-1, half))
    ).astype(BF)
    arrived = [
        ring.shift(grads[:, s * heads : (s + 1) * heads], -s) if s else grads[:, :heads]
        for s in range(ring.count)
    ]
    both = ring.place(arrived, -1)
    mine, theirs = both[: LEN // 2], swap_row(both[LEN // 2 :])
    mine, theirs = (v.reshape(-1, size, heads) for v in (mine, theirs))
    first = ring.core == 0
    mixed_grad = jnp.stack(
        [jnp.where(first, mine, theirs), jnp.where(first, theirs, mine)], axis=1
    ).reshape(LEN, heads)
    projected_grad = attend_back(qkv, mixed_grad, mixed, log_total, cos, sin)
    first_grad = ring.reduce_tokens(nt(projected_grad, attn_weight), nt(projected_grad, aw_other))

    block_output = (
        residual + ring.reduce_tokens(nn(hidden, down_weight), nn(hidden, dw_other))
    ).astype(BF)

    down_summed = reduce_weights_columns(hidden, co, ct)
    gate_summed = reduce_weights(tn(n2o, gate_grad).astype(BF), tn(n2t, gate_grad).astype(BF))
    up_summed = reduce_weights(tn(n2o, upper_grad).astype(BF), tn(n2t, upper_grad).astype(BF))
    ro, rt = ring.gather_tokens(residual_low)
    out_summed = reduce_weights(tn(mixed, ro).astype(BF), tn(mixed, rt).astype(BF))
    attn_summed = reduce_weights(
        tn(n1o, projected_grad).astype(BF), tn(n1t, projected_grad).astype(BF)
    )

    inputs = block_input.astype(F32)
    first_scale = lax.rsqrt(
        row_total(jnp.sum(inputs * inputs, axis=1, keepdims=True)) / width + norm_epsilon
    )
    first_hat = inputs * first_scale
    attn_part = jnp.sum(first_grad * first_hat, axis=0)
    weighted_first = first_grad * go1
    first_mean = row_total(jnp.sum(weighted_first * first_hat, axis=1, keepdims=True)) / width
    input_grad = residual_grad + first_scale * (weighted_first - first_hat * first_mean)
    attn_gain_grad, feed_gain_grad = lax.psum((attn_part, feed_part), ("dp", "col"))
    return (
        block_output,
        input_grad,
        attn_gain_grad,
        attn_summed,
        out_summed,
        feed_gain_grad,
        gate_summed,
        up_summed,
        down_summed,
    )


def reduce_weights_columns(hidden, co, ct):
    return reduce_weights(tn(hidden, co).astype(BF), tn(hidden, ct).astype(BF))


def solution(mesh):
    in_specs = (
        P(("dp", "col"), "row"),
        P("row"),
        P("row", "col"),
        P("col", "row"),
        P("row"),
        P("row", "col"),
        P("row", "col"),
        P("col", "row"),
        P(("dp", "col"), "row"),
    )
    out_specs = (
        P(("dp", "col"), "row"),
        P(("dp", "col"), "row"),
        P("row"),
        P("row", "col"),
        P("col", "row"),
        P("row"),
        P("row", "col"),
        P("row", "col"),
        P("col", "row"),
    )
    return jax.shard_map(shards, mesh=mesh, in_specs=in_specs, out_specs=out_specs, check_vma=False)
```

```python
import functools

import jax
import jax.numpy as jnp
from jax import lax
from jax.experimental import pallas as pl
from jax.experimental.pallas import tpu as pltpu
from jax.sharding import PartitionSpec as P

HD = 64
LEN = 1024
PAIR = 6 * HD
BLOCK = 256

norm_epsilon = 1e-05
rope_base = 130000.0
masked_score = -1e30
LOG2E = 1.4426950408889634
BF = jnp.bfloat16
F32 = jnp.float32
MIB = 1024 * 1024
SCALE = 0.5 * 1.15e9


def cost(us):
    return pl.CostEstimate(flops=int(us * SCALE), bytes_accessed=1, transcendentals=0)


def nn(left, right):
    return lax.dot_general(left, right, (((1,), (0,)), ((), ())), preferred_element_type=F32)


def nt(left, right):
    return lax.dot_general(left, right, (((1,), (1,)), ((), ())), preferred_element_type=F32)


def tn(left, right):
    return lax.dot_general(left, right, (((0,), (0,)), ((), ())), preferred_element_type=F32)


def params(mib):
    return pltpu.CompilerParams(vmem_limit_bytes=mib * MIB)


def rope_tables():
    steps_half = jnp.arange(HD // 2).astype(F32)
    frequency = rope_base ** (-2.0 * steps_half / HD)
    angles = jnp.arange(LEN).astype(F32)[:, None] * frequency[None, :]
    cos, sin = jnp.cos(angles), jnp.sin(angles)
    return (
        jnp.concatenate([cos] * 4, axis=1),
        jnp.concatenate([-sin, sin] * 2, axis=1),
    )


def project_kernel(xo, xt, go, gt, wo, wt, cos, sin, no, nt_, out, scales):
    @pl.when(pl.program_id(0) == 0)
    def _():
        rows = 256
        for i in range(LEN // rows):
            at = slice(i * rows, (i + 1) * rows)
            a = xo[at, :].astype(F32)
            b = xt[at, :].astype(F32)
            total = jnp.sum(a * a, axis=1, keepdims=True) + jnp.sum(b * b, axis=1, keepdims=True)
            scale = lax.rsqrt(total / (a.shape[1] + b.shape[1]) + norm_epsilon)
            no[at, :] = (a * scale * go[...]).astype(BF)
            nt_[at, :] = (b * scale * gt[...]).astype(BF)
            scales[at, :] = jnp.broadcast_to(scale, (rows, 128))

    proj = nn(no[...], wo[...]) + nn(nt_[...], wt[...])
    lane = lax.broadcasted_iota(jnp.int32, (LEN, 128), 1)
    low = (lane % HD) < HD // 2
    for piece in range(3):
        part = proj[:, piece * 128 : (piece + 1) * 128]
        swapped = jnp.where(low, pltpu.roll(part, 96, 1), pltpu.roll(part, 32, 1))
        turned = part * cos[...] + swapped * sin[...]
        if piece == 1:
            turned = jnp.where(lane < HD, part, turned)
        if piece == 2:
            turned = jnp.where(lane < HD, turned, part)
        out[:, piece * 128 : (piece + 1) * 128] = turned.astype(BF)


def project(xo, xt, go, gt, wo, wt, cos, sin):
    half, columns = wo.shape
    fixed = lambda shape: pl.BlockSpec(shape, lambda i: (0, 0))
    weight = pl.BlockSpec((half, PAIR), lambda i: (0, i))
    return pl.pallas_call(
        project_kernel,
        grid=(columns // PAIR,),
        in_specs=[fixed((LEN, half))] * 2
        + [fixed((1, half))] * 2
        + [weight] * 2
        + [fixed((LEN, 128))] * 2,
        out_specs=[fixed((LEN, half))] * 2
        + [pl.BlockSpec((LEN, PAIR), lambda i: (0, i)), fixed((LEN, 128))],
        out_shape=[jax.ShapeDtypeStruct((LEN, half), BF)] * 2
        + [jax.ShapeDtypeStruct((LEN, columns), BF), jax.ShapeDtypeStruct((LEN, 128), F32)],
        compiler_params=params(56),
        cost_estimate=cost(17),
    )(xo, xt, go, gt, wo, wt, cos, sin)


def head_parts(qkv, head):
    at = head * 3 * HD
    return qkv[:, at : at + HD], qkv[:, at + HD : at + 2 * HD], qkv[:, at + 2 * HD : at + 3 * HD]


def attend_kernel(qkv, out, log_total):
    scale = HD**-0.5 * LOG2E
    row = lax.broadcasted_iota(jnp.int32, (BLOCK, BLOCK), 0)
    col = lax.broadcasted_iota(jnp.int32, (BLOCK, BLOCK), 1)
    for head in range(2):
        q, k, v = head_parts(qkv, head)
        for i in range(LEN // BLOCK):
            start, end = i * BLOCK, (i + 1) * BLOCK
            scores = nt(q[start:end], k[:end])
            last = jnp.where(row >= col, scores[:, start:], masked_score)
            scores = jnp.concatenate([scores[:, :start], last], axis=1) if i else last
            peak = jnp.max(scores, axis=1, keepdims=True)
            probs = jnp.exp2((scores - peak) * scale)
            total = jnp.sum(probs, axis=1, keepdims=True)
            mixed = nn(probs.astype(BF), v[:end]) / total
            out[start:end, head * HD : (head + 1) * HD] = mixed.astype(BF)
            log_total[start:end, head * HD : (head + 1) * HD] = jnp.broadcast_to(
                peak * scale + jnp.log2(total), (BLOCK, HD)
            )


def attend(qkv, group, groups):
    pairs = qkv.shape[1] // PAIR // groups
    narrow = pl.BlockSpec((LEN, 2 * HD), lambda i: (0, i))
    return pl.pallas_call(
        attend_kernel,
        grid=(pairs,),
        in_specs=[pl.BlockSpec((LEN, PAIR), lambda i: (0, group * pairs + i))],
        out_specs=[narrow, narrow],
        out_shape=[
            jax.ShapeDtypeStruct((LEN, pairs * 2 * HD), BF),
            jax.ShapeDtypeStruct((LEN, pairs * 2 * HD), F32),
        ],
        compiler_params=params(48),
        cost_estimate=cost(4 * pairs),
    )(qkv)


def attend_back_kernel(qkv, grad, mixed, log_total, cos, sin, out):
    scale = HD**-0.5 * LOG2E
    row = lax.broadcasted_iota(jnp.int32, (BLOCK, BLOCK), 0)
    col = lax.broadcasted_iota(jnp.int32, (BLOCK, BLOCK), 1)
    blocks = LEN // BLOCK
    totals = jnp.transpose(log_total[...])
    product = jnp.transpose(grad[...].astype(F32) * mixed[...].astype(F32))
    cosines, sines = cos[:, :HD], sin[:, :HD]

    def unturn(part, start, end):
        swapped = jnp.concatenate([part[:, HD // 2 :], part[:, : HD // 2]], axis=1)
        return (part * cosines[start:end] - swapped * sines[start:end]).astype(BF)

    for head in range(2):
        q, k, v = head_parts(qkv, head)
        at = head * 3 * HD
        g = grad[:, head * HD : (head + 1) * HD]
        total = totals[head * HD : head * HD + 1]
        center = jnp.sum(product[head * HD : (head + 1) * HD], axis=0, keepdims=True)
        query_grad = [None] * blocks
        for j in range(blocks):
            start, end = j * BLOCK, (j + 1) * BLOCK
            scores = nt(k[start:end], q[start:])
            probs = jnp.exp2(scores * scale - total[:, start:])
            first = jnp.where(col >= row, probs[:, :BLOCK], 0.0)
            probs = jnp.concatenate([first, probs[:, BLOCK:]], axis=1) if end < LEN else first
            out[start:end, at + 2 * HD : at + 3 * HD] = nn(probs.astype(BF), g[start:]).astype(BF)
            prob_grad = nt(v[start:end], g[start:])
            score_grad = (probs * (prob_grad - center[:, start:])).astype(BF)
            key_grad = nn(score_grad, q[start:]) * (HD**-0.5)
            out[start:end, at + HD : at + 2 * HD] = unturn(key_grad, start, end)
            term = tn(k[start:end], score_grad)
            for b in range(j, blocks):
                here = term[:, (b - j) * BLOCK : (b - j + 1) * BLOCK]
                query_grad[b] = here if query_grad[b] is None else query_grad[b] + here
        for b in range(blocks):
            start, end = b * BLOCK, (b + 1) * BLOCK
            out[start:end, at : at + HD] = unturn(
                jnp.transpose(query_grad[b]) * (HD**-0.5), start, end
            )


def attend_back(qkv, grad, mixed, log_total, cos, sin):
    pairs = qkv.shape[1] // PAIR
    wide = pl.BlockSpec((LEN, PAIR), lambda i: (0, i))
    narrow = pl.BlockSpec((LEN, 2 * HD), lambda i: (0, i))
    fixed = pl.BlockSpec((LEN, 128), lambda i: (0, 0))
    return pl.pallas_call(
        attend_back_kernel,
        grid=(pairs,),
        in_specs=[wide, narrow, narrow, narrow, fixed, fixed],
        out_specs=wide,
        out_shape=jax.ShapeDtypeStruct((LEN, pairs * PAIR), BF),
        compiler_params=params(56),
        cost_estimate=cost(5 * pairs),
    )(qkv, grad, mixed, log_total, cos, sin)


def mix_kernel(start, groups, count, last, *refs):
    mixed = refs[:count]
    wo, wt, ao, at = refs[count : count + 4]
    a = ao[...].astype(F32)
    b = at[...].astype(F32)
    for index in range(count):
        left = mixed[index][...]
        depth = left.shape[1]
        step, low = start + index // groups, index % groups * depth
        a = a + nn(left, wo[step, low : low + depth, :])
        b = b + nn(left, wt[step, low : low + depth, :])
    if not last:
        ro, rt = refs[count + 4 :]
    else:
        go, gt, ro, rt, no, nt_ = refs[count + 4 :]
        total = jnp.sum(a * a, axis=1, keepdims=True) + jnp.sum(b * b, axis=1, keepdims=True)
        scale = lax.rsqrt(total / (a.shape[1] + b.shape[1]) + norm_epsilon)
        no[...] = (a * scale * go[...]).astype(BF)
        nt_[...] = (b * scale * gt[...]).astype(BF)
    ro[...] = a
    rt[...] = b


def mix(mixed, wo, wt, ao, at, start, gains=None):
    depth, half = wo.shape[1:]
    count = len(mixed)
    groups = depth // mixed[0].shape[1]
    steps = count // groups
    rows = 256
    if start % steps == 0:
        weight = pl.BlockSpec((steps, depth, half), lambda i: (start // steps, 0, 0))
        offset = 0
    else:
        weight = pl.BlockSpec(wo.shape, lambda i: (0, 0, 0))
        offset = start
    left = pl.BlockSpec((rows, depth // groups), lambda i: (i, 0))
    part = pl.BlockSpec((rows, half), lambda i: (i, 0))
    gain = pl.BlockSpec((1, half), lambda i: (0, 0))
    last = gains is not None
    more = list(gains) if last else []
    return pl.pallas_call(
        functools.partial(mix_kernel, offset, groups, count, last),
        grid=(LEN // rows,),
        in_specs=[left] * count + [weight] * 2 + [part] * 2 + [gain] * len(more),
        out_specs=[part] * (4 if last else 2),
        out_shape=[jax.ShapeDtypeStruct((LEN, half), F32)] * 2
        + [jax.ShapeDtypeStruct((LEN, half), BF)] * (2 if last else 0),
        compiler_params=params(56),
        cost_estimate=cost(3 * count),
    )(*mixed, wo, wt, ao, at, *more)


def feed_kernel(no, nt_, back, gwo, gwt, uwo, uwt, hidden, gate_grad, upper_grad):
    gate = nn(no[...], gwo[...]) + nn(nt_[...], gwt[...])
    upper = nn(no[...], uwo[...]) + nn(nt_[...], uwt[...])
    sigmoid = 1.0 / (1.0 + jnp.exp(-gate))
    silu = gate * sigmoid
    hidden[...] = (silu * upper).astype(BF)
    hidden_grad = back[...]
    gate_grad[...] = (hidden_grad * upper * sigmoid * (1.0 + gate * (1.0 - sigmoid))).astype(BF)
    upper_grad[...] = (hidden_grad * silu).astype(BF)


def feed(no, nt_, back, gwo, gwt, uwo, uwt):
    half, units = gwo.shape
    tokens = pl.BlockSpec((LEN, half), lambda i: (0, 0))
    weight = pl.BlockSpec((half, BLOCK), lambda i: (0, i))
    out = pl.BlockSpec((LEN, BLOCK), lambda i: (0, i))
    return pl.pallas_call(
        feed_kernel,
        grid=(units // BLOCK,),
        in_specs=[tokens] * 2 + [out] + [weight] * 4,
        out_specs=[out] * 3,
        out_shape=[jax.ShapeDtypeStruct((LEN, units), BF)] * 3,
        compiler_params=params(60),
        cost_estimate=cost(26),
    )(no, nt_, back, gwo, gwt, uwo, uwt)


def product_kernel(kind, terms, more, *refs):
    lefts, rights = refs[:terms], refs[terms : 2 * terms]
    out = refs[2 * terms + more]
    if kind == "tn":
        turned = refs[2 * terms + more + 1 :]

        @pl.when(pl.program_id(0) == 0)
        def _():
            for left, kept in zip(lefts, turned):
                kept[...] = left[...].T

        lefts = turned
    dot = nt if kind == "nt" else nn
    total = refs[2 * terms][...].astype(F32) if more else None
    for left, right in zip(lefts, rights):
        term = dot(left[...], right[...])
        total = term if total is None else total + term
    out[...] = total.astype(out.dtype)


def product(kind, lefts, rights, kind_out=BF, extra=None, part=None, tile=512):
    which, parts = part or (0, 1)
    rows = lefts[0].shape[1 if kind == "tn" else 0]
    columns = rights[0].shape[0 if kind == "nt" else 1] // parts
    tile = min(tile, columns)
    first = which * (columns // tile)
    fixed = [pl.BlockSpec(v.shape, lambda i: (0, 0)) for v in lefts]
    if kind == "nt":
        moving = [pl.BlockSpec((tile, v.shape[1]), lambda i: (first + i, 0)) for v in rights]
    else:
        moving = [pl.BlockSpec((v.shape[0], tile), lambda i: (0, first + i)) for v in rights]
    out = pl.BlockSpec((rows, tile), lambda i: (0, i))
    more = [] if extra is None else [extra]
    return pl.pallas_call(
        functools.partial(product_kernel, kind, len(lefts), len(more)),
        grid=(columns // tile,),
        in_specs=fixed + moving + [out] * len(more),
        out_specs=out,
        out_shape=jax.ShapeDtypeStruct((rows, columns), kind_out),
        scratch_shapes=[pltpu.VMEM(v.shape[::-1], BF) for v in lefts] if kind == "tn" else [],
        compiler_params=params(60),
        cost_estimate=cost(1 + len(lefts) * lefts[0].size * columns / 3.4e8),
    )(*lefts, *rights, *more)


def beside_kernel(tiles, more, *refs):
    left, first, second = refs[:3]
    out, turned = refs[3 + more :]
    at = pl.program_id(0)

    @pl.when(at == 0)
    def _():
        turned[...] = left[...].T

    def store(right):
        total = nn(turned[...], right[...])
        if more:
            total = total + refs[3][...].astype(F32)
        out[...] = total.astype(out.dtype)

    @pl.when(at < tiles)
    def _():
        store(first)

    @pl.when(at >= tiles)
    def _():
        store(second)


def product_beside(left, first, second, extra=None, tile=512):
    depth, rows = left.shape
    columns = first.shape[1]
    tile = min(tile, columns)
    tiles = columns // tile
    out = pl.BlockSpec((rows, tile), lambda i: (0, i))
    more = [] if extra is None else [extra]
    return pl.pallas_call(
        functools.partial(beside_kernel, tiles, len(more)),
        grid=(2 * tiles,),
        in_specs=[
            pl.BlockSpec(left.shape, lambda i: (0, 0)),
            pl.BlockSpec((depth, tile), lambda i: (0, jnp.minimum(i, tiles - 1))),
            pl.BlockSpec((depth, tile), lambda i: (0, jnp.maximum(i - tiles, 0))),
        ]
        + [out] * len(more),
        out_specs=out,
        out_shape=jax.ShapeDtypeStruct((rows, 2 * columns), BF),
        scratch_shapes=[pltpu.VMEM((rows, depth), BF)],
        compiler_params=params(60),
        cost_estimate=cost(16),
    )(left, first, second, *more)


def swap_row(values):
    return lax.ppermute(values, "row", [(0, 1), (1, 0)])


class Ring:
    def __init__(self):
        count = lax.axis_size("col")
        self.count = count
        self.order = list(range(0, count, 2)) + list(range(count - 1, 0, -2))
        index = lax.axis_index("col")
        self.here = jnp.where(index % 2 == 0, index // 2, count - 1 - index // 2)
        self.core = lax.axis_index("row")

    def shift(self, values, by=1):
        count, order = self.count, self.order
        pairs = [(order[p], order[(p + by) % count]) for p in range(count)]
        return lax.ppermute(values, "col", pairs)

    def owner(self, back):
        count = self.count
        at = (self.here + (2 * count - back)) % count
        return jnp.where(at < count // 2, 2 * at, 2 * (count - 1 - at) + 1)

    def split(self, owner):
        per = self.count // 2
        return owner // per, owner % per

    def place(self, halves, direction):
        rows, columns = halves[0][0].shape
        whole = rows * len(halves)
        out = jnp.zeros((self.count * whole, columns), halves[0][0].dtype)
        for low, blocks in enumerate(halves):
            for step, block in enumerate(blocks):
                sequence, at = self.split(self.owner(direction * step))
                slot = jnp.where(sequence == self.core, 0, self.count // 2) + at
                out = lax.dynamic_update_slice(out, block, (slot * whole + low * rows, 0))
        return out

    def term(self, own, other, back):
        rows = own.shape[0] * 2 // self.count
        sequence, at = self.split(self.owner(back))
        take = lambda values: lax.dynamic_slice_in_dim(values, at * rows, rows, 0)
        return jnp.where(sequence == self.core, take(own), take(other))


def halve(values, bit, axis):
    size = values.shape[axis] // 2
    return lax.dynamic_slice_in_dim(values, bit * size, size, axis)


def join(values, others, bit, axis):
    first = jnp.where(bit == 0, values, others)
    second = jnp.where(bit == 0, others, values)
    return jnp.concatenate([first, second], axis=axis)


class Square:
    def __init__(self):
        index = lax.axis_index("dp")
        bits = (index % 2, index // 2)
        hops = tuple(
            lambda v, flip=flip: lax.ppermute(v, "dp", [(i, i ^ flip) for i in range(4)])
            for flip in (1, 2)
        )
        self.bits, self.hops = bits, hops
        self.index = index

    def send(self, parts, phase, axis):
        got = []
        for which, addends in enumerate(parts):
            turn = which ^ (phase - 1)
            out = sum(halve(v, 1 - self.bits[turn], axis).astype(F32) for v in addends)
            got.append(self.hops[turn](out.astype(BF)))
        return got

    def add(self, parts, got, phase, axis, kind=F32):
        kept = []
        for which, addends in enumerate(parts):
            turn = which ^ (phase - 1)
            out = sum(halve(v, self.bits[turn], axis).astype(F32) for v in addends)
            kept.append((out + got[which].astype(F32)).astype(kind))
        return kept

    def hop(self, parts, phase):
        return [self.hops[which ^ (phase - 1)](v) for which, v in enumerate(parts)]

    def join(self, parts, got, phase, axis):
        return [
            join(v, got[which], self.bits[which ^ (phase - 1)], axis)
            for which, v in enumerate(parts)
        ]


def row_total(values):
    return values + swap_row(values)


def shards(
    block_input,
    attn_gain,
    attn_weight,
    out_weight,
    feed_gain,
    gate_weight,
    up_weight,
    down_weight,
    out_cotangent,
):
    ring = Ring()
    square = Square()
    count, core = ring.count, ring.core
    rows, half = block_input.shape
    size = rows // 2
    width = 2 * half
    own_sequence, own_at = ring.split(lax.axis_index("col"))
    local = own_sequence == core

    steps = count - 1
    s = dict(
        x=block_input,
        cot=out_cotangent,
        aw=attn_weight,
        gw=gate_weight,
        uw=up_weight,
        dw=down_weight,
        gains=jnp.concatenate([attn_gain[None, :], feed_gain[None, :]], axis=0),
    )

    def tie(*held):
        kept = {name: s.pop(name) for name in held if name in s}
        fixed = lax.optimization_barrier(dict(s))
        s.clear()
        s.update(fixed)
        s.update(kept)

    def push(name):
        s[name] = s[name] + [ring.shift(s[name][-1])]

    def reduce_step(name, k):
        term = ring.term(s[name + "_own"], s[name + "_other"], k + 1)
        if k:
            term = (s[name].astype(F32) + term.astype(F32)).astype(BF)
        s[name] = ring.shift(term)

    def reduce_end(name):
        own, other = s.pop(name + "_own"), s.pop(name + "_other")
        return s.pop(name).astype(F32) + ring.term(own, other, count).astype(F32)

    quarter = out_weight.shape[0] // 4
    s["qs"] = [lax.dynamic_slice_in_dim(out_weight, square.index * quarter, quarter, 0)]
    s["xs"], s["cs"] = [s["x"]], [s["cot"]]
    for k in range(steps):
        push("xs")
        if k == 0:
            s["aw2"] = swap_row(s["aw"])
            s["gains2"] = swap_row(s["gains"])
            s["cos"], s["sin"] = rope_tables()
            inputs = s["x"].astype(F32)
            squares = jnp.sum(inputs * inputs, axis=1)
            s["first_scale"] = lax.rsqrt(row_total(squares) / width + norm_epsilon)
        if k == 1:
            s["gw2"] = swap_row(s["gw"])
        if k == 2:
            s["uw2"] = swap_row(s["uw"])
        if k >= 2 and len(s["qs"]) < count:
            push("qs")
        tie()

    push("cs")
    if len(s["qs"]) < count:
        push("qs")
    both = ring.place([s.pop("xs")], 1)
    s["xo"] = both[:LEN]
    s["xt"] = swap_row(both[LEN:])
    s["n1o"], s["n1t"], s["qkv"], s["scale1"] = project(
        s["xo"],
        s["xt"],
        s["gains"][:1],
        s["gains2"][:1],
        s["aw"],
        s["aw2"],
        s["cos"],
        s["sin"],
    )
    tie()
    for k in range(1, steps - 1):
        push("cs")
        if len(s["qs"]) < count:
            push("qs")
        if k == 1:
            mixed, s["log_total"] = attend(s["qkv"], 0, 1)
            s["mixed"] = [mixed]
        tie()

    push("mixed")
    push("cs")
    s["dw2"] = swap_row(s["dw"])
    held = jnp.stack(s.pop("qs"), axis=0)
    s["ow"] = [held[: count // 2], held[count // 2 :]]
    s["ow_got"] = square.hop(s["ow"], 1)
    tie()
    push("mixed")
    s["ow"] = square.join(s["ow"], s.pop("ow_got"), 1, 1)
    s["ow_got"] = square.hop(s["ow"], 2)
    both = ring.place([s.pop("cs")], 1)
    s["co"] = both[:LEN]
    s["ct"] = swap_row(both[LEN:])
    s["back"] = product("nt", [s["co"]], [s["dw"]], F32)
    s["back"] = product("nt", [s["ct"]], [s["dw2"]], F32, s["back"])
    tie()
    for k in range(2, steps):
        push("mixed")
        if k == 2:
            first, second = square.join(s.pop("ow"), s.pop("ow_got"), 2, 1)
            shape = second.shape
            second = second.reshape(shape[0], 2, 2, quarter, half).swapaxes(1, 2).reshape(shape)
            s["owo"] = jnp.concatenate([first, second], axis=0)
            s["owt"] = swap_row(s["owo"])
            s["ro"], s["rt"] = mix(s["mixed"][:3], s["owo"], s["owt"], s["xo"], s["xt"], 0)
        tie()

    gains, gains2 = s["gains"], s["gains2"]
    s["ro"], s["rt"], s["n2o"], s["n2t"] = mix(
        s["mixed"][3:], s["owo"], s["owt"], s["ro"], s["rt"], 3, (gains[1:], gains2[1:])
    )
    s["hidden"], s["gg"], s["ug"] = feed(
        s["n2o"], s["n2t"], s.pop("back"), s["gw"], s["gw2"], s["uw"], s["uw2"]
    )
    tie()
    s["dn_other"] = product("nn", [s["hidden"]], [s.pop("dw2")])
    tie()
    s["dn_other"] = swap_row(s["dn_other"])
    s["dn_own"] = product("nn", [s["hidden"]], [s.pop("dw")])
    tie()
    reduce_step("dn", 0)
    s["down_other"] = product("tn", [s["hidden"]], [s.pop("ct")])
    tie("dn")
    s["down_other"] = swap_row(s["down_other"])
    s["sg_other"] = product("nt", [s["gg"], s["ug"]], [s.pop("gw2"), s.pop("uw2")])
    tie()
    s["sg_other"] = swap_row(s["sg_other"])
    s["down"] = product("tn", [s.pop("hidden")], [s.pop("co")], extra=s.pop("down_other"))
    tie()
    s["down"] = lax.psum_scatter(s["down"], "dp", scatter_dimension=0, tiled=True)
    s["sg_own"] = product("nt", [s["gg"], s["ug"]], [s.pop("gw"), s.pop("uw")])
    tie("down")

    take = lambda v: lax.dynamic_slice_in_dim(v, own_at * rows, rows, 0)
    reduce_step("sg", 0)
    s["both_other"] = product_beside(s.pop("n2t"), s["gg"], s["ug"])
    s["res"] = jnp.where(local, take(s.pop("ro")), swap_row(take(s.pop("rt"))))
    tie()
    s["down"] = lax.all_gather(s["down"], "dp", axis=0, tiled=True)
    reduce_step("sg", 1)
    s["both_other"] = swap_row(s["both_other"])
    residual = s["res"]
    squares = row_total(jnp.sum(residual * residual, axis=1))
    s["second_scale"] = lax.rsqrt(squares / width + norm_epsilon)

    def tokens(which):
        part = [
            lax.dynamic_slice_in_dim(v, own_at * rows + which * size, size, 0)
            for v in s["mixed"]
        ]
        return jnp.concatenate(
            [v[:, q * quarter : (q + 1) * quarter] for q in range(4) for v in part], axis=1
        )

    s["mixed_rows"] = jnp.where(local, tokens(core), swap_row(tokens(1 - core)))
    s["mixed"] = s["mixed"][0]
    s["both"] = product_beside(s.pop("n2o"), s.pop("gg"), s.pop("ug"), s.pop("both_other"))
    tie("down")
    for k in range(2, steps):
        reduce_step("sg", k)
        if k == 2:
            s["both"] = lax.psum_scatter(s["both"], "dp", scatter_dimension=0, tiled=True)
        tie("both", "down")

    reduce_step("dn", 1)
    second_grad = reduce_end("sg")
    second_hat = s["res"] * s["second_scale"][:, None]
    s["feed_part"] = jnp.sum(second_grad * second_hat, axis=0, keepdims=True)
    weighted = second_grad * s["gains"][1:]
    second_mean = row_total(jnp.sum(weighted * second_hat, axis=1)) / width
    s["residual_grad"] = s["cot"].astype(F32) + s["second_scale"][:, None] * (
        weighted - second_hat * second_mean[:, None]
    )
    low = s["residual_grad"].astype(BF)
    s["low_own"] = lax.dynamic_slice_in_dim(low, core * size, size, 0)
    s["low_other"] = swap_row(lax.dynamic_slice_in_dim(low, (1 - core) * size, size, 0))
    heads = s["mixed"].shape[1]
    grads = product(
        "nt",
        [s["low_own"], s["low_other"]],
        [s.pop("owo").reshape(-1, half), s.pop("owt").reshape(-1, half)],
    )
    s["grads"] = [grads[:, i * heads : (i + 1) * heads] for i in range(count)]
    tie("both")

    s["grads"] = [ring.shift(v, -i) if i else v for i, v in enumerate(s["grads"])]
    other = swap_row(product("tn", [s["mixed_rows"]], [s.pop("low_other")]))
    s["out"] = product("tn", [s.pop("mixed_rows")], [s.pop("low_own")], extra=other)
    tie("both")

    for k in range(2, steps):
        reduce_step("dn", k)
        if k < steps - 1:
            tie("both", "down")
    s["out"] = lax.psum_scatter(s["out"], "dp", scatter_dimension=0, tiled=True)
    both = ring.place([s.pop("grads")], -1)
    mine, theirs = both[: LEN // 2], swap_row(both[LEN // 2 :])
    mine, theirs = (v.reshape(-1, size, heads) for v in (mine, theirs))
    grad = jnp.stack(
        [jnp.where(core == 0, mine, theirs), jnp.where(core == 0, theirs, mine)], axis=1
    ).reshape(LEN, heads)
    s["pg"] = attend_back(
        s.pop("qkv"), grad, s.pop("mixed"), s.pop("log_total"), s.pop("cos"), s.pop("sin")
    )
    tie("out")
    s["both"] = lax.all_gather(s["both"], "dp", axis=0, tiled=True)
    s["fg_local"] = product("nt", [s["pg"]], [s.pop("aw2")])
    s["attn_other"] = product("tn", [s.pop("n1t")], [s["pg"]], tile=PAIR)
    tie("both", "out")
    s["fg_other"] = swap_row(s["fg_local"])
    s["attn_other"] = swap_row(s["attn_other"])
    s["fg_own"] = product("nt", [s["pg"]], [s.pop("aw")])
    tie("both")

    def split(name):
        values = s[name]
        cut = values.shape[0] // 2
        s[name] = [[values[:cut]], [values[cut:]]]
        s[name + "_got"] = square.send(s[name], 1, 0)

    def phase(name, which):
        got = s.pop(name + "_got")
        if which == 2:
            s[name] = [[v] for v in square.add(s[name], got, 1, 0)]
            s[name + "_got"] = square.send(s[name], 2, 0)
        if which == 3:
            s[name] = square.add(s[name], got, 2, 0, BF)
            s[name + "_got"] = square.hop(s[name], 2)
        if which == 4:
            s[name] = square.join(s[name], got, 2, 0)
            s[name + "_got"] = square.hop(s[name], 1)
        if which == 5:
            halves = square.join(s[name], got, 1, 0)
            s[name] = jnp.concatenate(halves, axis=0).astype(F32)

    def out_step(k):
        term = s["out"][(k + 1) % count]
        if k:
            term = (s["out_ring"].astype(F32) + term.astype(F32)).astype(BF)
        s["out_ring"] = ring.shift(term)

    reduce_step("fg", 0)
    s["attn"] = product("tn", [s.pop("n1o")], [s.pop("pg")], extra=s.pop("attn_other"), tile=PAIR)
    scale1 = s.pop("scale1")[:, :1]
    part = lambda grad, inputs: jnp.sum(
        grad.astype(F32) * (inputs.astype(F32) * scale1), axis=0, keepdims=True
    )
    other = swap_row(part(s.pop("fg_local"), s.pop("xt")))
    s["parts"] = jnp.concatenate(
        [part(s["fg_own"], s.pop("xo")) + other, s.pop("feed_part")], axis=0
    )
    tie("both", "out")
    reduce_step("fg", 1)
    split("attn")
    s["parts"] = s["parts"] + square.hops[0](s["parts"])
    s["output"] = (s.pop("res") + reduce_end("dn")).astype(BF)
    s["down"] = s["down"].astype(F32)
    tie("both")
    s["out"] = s["out"].reshape(count, quarter, half)
    for k in range(2, steps):
        reduce_step("fg", k)
        if k == 2:
            phase("attn", 2)
            out_step(0)
            s["parts"] = s["parts"] + square.hops[1](s["parts"])
            tie("both", "fg")
            phase("attn", 3)
            out_step(1)
            parts = s.pop("parts")
            s["parts"] = sum([ring.shift(parts, i) for i in range(1, count)], parts)
        tie("both")
    phase("attn", 4)
    for k in range(2, steps):
        out_step(k)
    first_grad = reduce_end("fg")
    scale = s["first_scale"][:, None]
    first_hat = s["x"].astype(F32) * scale
    weighted = first_grad * s["gains"][:1]
    first_mean = row_total(jnp.sum(weighted * first_hat, axis=1)) / width
    s["input"] = s["residual_grad"] + scale * (weighted - first_hat * first_mean[:, None])
    tie("both")
    out = (s.pop("out_ring").astype(F32) + s["out"][0].astype(F32)).astype(BF)
    s["out"] = join(out, square.hops[0](out), square.bits[0], 0)
    tie("both")
    s["out"] = join(s["out"], square.hops[1](s["out"]), square.bits[1], 0).astype(F32)
    phase("attn", 5)
    tie()
    units = gate_weight.shape[1]
    s["gate"] = s["both"][:, :units].astype(F32)
    s["up"] = s.pop("both")[:, units:].astype(F32)
    return (
        s["output"],
        s["input"],
        s["parts"][0],
        s["attn"],
        s["out"],
        s["parts"][1],
        s["gate"],
        s["up"],
        s["down"],
    )


def solution(mesh):
    in_specs = (
        P(("dp", "col"), "row"),
        P("row"),
        P("row", "col"),
        P("col", "row"),
        P("row"),
        P("row", "col"),
        P("row", "col"),
        P("col", "row"),
        P(("dp", "col"), "row"),
    )
    out_specs = (
        P(("dp", "col"), "row"),
        P(("dp", "col"), "row"),
        P("row"),
        P("row", "col"),
        P("col", "row"),
        P("row"),
        P("row", "col"),
        P("row", "col"),
        P("col", "row"),
    )
    return jax.shard_map(shards, mesh=mesh, in_specs=in_specs, out_specs=out_specs, check_vma=False)
```

```python
import functools

import jax
import jax.numpy as jnp
from jax import lax
from jax.experimental import pallas as pl
from jax.experimental.pallas import tpu as pltpu
from jax.sharding import PartitionSpec as P

HD = 64
LEN = 1024
PAIR = 6 * HD
BLOCK = 256

norm_epsilon = 1e-05
rope_base = 130000.0
masked_score = -1e30
LOG2E = 1.4426950408889634
BF = jnp.bfloat16
F32 = jnp.float32
MIB = 1024 * 1024
SCALE = 0.5 * 1.15e9


def cost(us):
    return pl.CostEstimate(flops=int(us * SCALE), bytes_accessed=1, transcendentals=0)


def nn(left, right):
    return lax.dot_general(left, right, (((1,), (0,)), ((), ())), preferred_element_type=F32)


def nt(left, right):
    return lax.dot_general(left, right, (((1,), (1,)), ((), ())), preferred_element_type=F32)


def tn(left, right):
    return lax.dot_general(left, right, (((0,), (0,)), ((), ())), preferred_element_type=F32)


def params(mib):
    return pltpu.CompilerParams(vmem_limit_bytes=mib * MIB)


def rope_tables():
    steps_half = jnp.arange(HD // 2).astype(F32)
    frequency = rope_base ** (-2.0 * steps_half / HD)
    angles = jnp.arange(LEN).astype(F32)[:, None] * frequency[None, :]
    cos, sin = jnp.cos(angles), jnp.sin(angles)
    return (
        jnp.concatenate([cos] * 4, axis=1),
        jnp.concatenate([-sin, sin] * 2, axis=1),
    )


def project_kernel(xo, xt, go, gt, wo, wt, cos, sin, no, nt_, out, scales):
    @pl.when(pl.program_id(0) == 0)
    def _():
        rows = 256
        for i in range(LEN // rows):
            at = slice(i * rows, (i + 1) * rows)
            a = xo[at, :].astype(F32)
            b = xt[at, :].astype(F32)
            total = jnp.sum(a * a, axis=1, keepdims=True) + jnp.sum(b * b, axis=1, keepdims=True)
            scale = lax.rsqrt(total / (a.shape[1] + b.shape[1]) + norm_epsilon)
            no[at, :] = (a * scale * go[...]).astype(BF)
            nt_[at, :] = (b * scale * gt[...]).astype(BF)
            scales[at, :] = jnp.broadcast_to(scale, (rows, 128))

    proj = nn(no[...], wo[...]) + nn(nt_[...], wt[...])
    lane = lax.broadcasted_iota(jnp.int32, (LEN, 128), 1)
    low = (lane % HD) < HD // 2
    for piece in range(3):
        part = proj[:, piece * 128 : (piece + 1) * 128]
        swapped = jnp.where(low, pltpu.roll(part, 96, 1), pltpu.roll(part, 32, 1))
        turned = part * cos[...] + swapped * sin[...]
        if piece == 1:
            turned = jnp.where(lane < HD, part, turned)
        if piece == 2:
            turned = jnp.where(lane < HD, turned, part)
        out[:, piece * 128 : (piece + 1) * 128] = turned.astype(BF)


def project(xo, xt, go, gt, wo, wt, cos, sin):
    half, columns = wo.shape
    fixed = lambda shape: pl.BlockSpec(shape, lambda i: (0, 0))
    weight = pl.BlockSpec((half, PAIR), lambda i: (0, i))
    return pl.pallas_call(
        project_kernel,
        grid=(columns // PAIR,),
        in_specs=[fixed((LEN, half))] * 2
        + [fixed((1, half))] * 2
        + [weight] * 2
        + [fixed((LEN, 128))] * 2,
        out_specs=[fixed((LEN, half))] * 2
        + [pl.BlockSpec((LEN, PAIR), lambda i: (0, i)), fixed((LEN, 128))],
        out_shape=[jax.ShapeDtypeStruct((LEN, half), BF)] * 2
        + [jax.ShapeDtypeStruct((LEN, columns), BF), jax.ShapeDtypeStruct((LEN, 128), F32)],
        compiler_params=params(56),
        cost_estimate=cost(17),
    )(xo, xt, go, gt, wo, wt, cos, sin)


def head_parts(qkv, head):
    at = head * 3 * HD
    return qkv[:, at : at + HD], qkv[:, at + HD : at + 2 * HD], qkv[:, at + 2 * HD : at + 3 * HD]


def attend_kernel(qkv, out, log_total):
    scale = HD**-0.5 * LOG2E
    row = lax.broadcasted_iota(jnp.int32, (BLOCK, BLOCK), 0)
    col = lax.broadcasted_iota(jnp.int32, (BLOCK, BLOCK), 1)
    for head in range(2):
        q, k, v = head_parts(qkv, head)
        for i in range(LEN // BLOCK):
            start, end = i * BLOCK, (i + 1) * BLOCK
            scores = nt(q[start:end], k[:end])
            last = jnp.where(row >= col, scores[:, start:], masked_score)
            scores = jnp.concatenate([scores[:, :start], last], axis=1) if i else last
            peak = jnp.max(scores, axis=1, keepdims=True)
            probs = jnp.exp2((scores - peak) * scale)
            total = jnp.sum(probs, axis=1, keepdims=True)
            mixed = nn(probs.astype(BF), v[:end]) / total
            out[start:end, head * HD : (head + 1) * HD] = mixed.astype(BF)
            log_total[start:end, head * HD : (head + 1) * HD] = jnp.broadcast_to(
                peak * scale + jnp.log2(total), (BLOCK, HD)
            )


def attend(qkv, group, groups):
    pairs = qkv.shape[1] // PAIR // groups
    narrow = pl.BlockSpec((LEN, 2 * HD), lambda i: (0, i))
    return pl.pallas_call(
        attend_kernel,
        grid=(pairs,),
        in_specs=[pl.BlockSpec((LEN, PAIR), lambda i: (0, group * pairs + i))],
        out_specs=[narrow, narrow],
        out_shape=[
            jax.ShapeDtypeStruct((LEN, pairs * 2 * HD), BF),
            jax.ShapeDtypeStruct((LEN, pairs * 2 * HD), F32),
        ],
        compiler_params=params(48),
        cost_estimate=cost(4 * pairs),
    )(qkv)


def attend_back_kernel(qkv, grad, mixed, log_total, cos, sin, out):
    scale = HD**-0.5 * LOG2E
    row = lax.broadcasted_iota(jnp.int32, (BLOCK, BLOCK), 0)
    col = lax.broadcasted_iota(jnp.int32, (BLOCK, BLOCK), 1)
    blocks = LEN // BLOCK
    totals = jnp.transpose(log_total[...])
    product = jnp.transpose(grad[...].astype(F32) * mixed[...].astype(F32))
    cosines, sines = cos[:, :HD], sin[:, :HD]

    def unturn(part, start, end):
        swapped = jnp.concatenate([part[:, HD // 2 :], part[:, : HD // 2]], axis=1)
        return (part * cosines[start:end] - swapped * sines[start:end]).astype(BF)

    for head in range(2):
        q, k, v = head_parts(qkv, head)
        at = head * 3 * HD
        g = grad[:, head * HD : (head + 1) * HD]
        total = totals[head * HD : head * HD + 1]
        center = jnp.sum(product[head * HD : (head + 1) * HD], axis=0, keepdims=True)
        query_grad = [None] * blocks
        for j in range(blocks):
            start, end = j * BLOCK, (j + 1) * BLOCK
            scores = nt(k[start:end], q[start:])
            probs = jnp.exp2(scores * scale - total[:, start:])
            first = jnp.where(col >= row, probs[:, :BLOCK], 0.0)
            probs = jnp.concatenate([first, probs[:, BLOCK:]], axis=1) if end < LEN else first
            out[start:end, at + 2 * HD : at + 3 * HD] = nn(probs.astype(BF), g[start:]).astype(BF)
            prob_grad = nt(v[start:end], g[start:])
            score_grad = (probs * (prob_grad - center[:, start:])).astype(BF)
            key_grad = nn(score_grad, q[start:]) * (HD**-0.5)
            out[start:end, at + HD : at + 2 * HD] = unturn(key_grad, start, end)
            term = tn(k[start:end], score_grad)
            for b in range(j, blocks):
                here = term[:, (b - j) * BLOCK : (b - j + 1) * BLOCK]
                query_grad[b] = here if query_grad[b] is None else query_grad[b] + here
        for b in range(blocks):
            start, end = b * BLOCK, (b + 1) * BLOCK
            out[start:end, at : at + HD] = unturn(
                jnp.transpose(query_grad[b]) * (HD**-0.5), start, end
            )


def attend_back(qkv, grad, mixed, log_total, cos, sin):
    pairs = qkv.shape[1] // PAIR
    wide = pl.BlockSpec((LEN, PAIR), lambda i: (0, i))
    narrow = pl.BlockSpec((LEN, 2 * HD), lambda i: (0, i))
    fixed = pl.BlockSpec((LEN, 128), lambda i: (0, 0))
    return pl.pallas_call(
        attend_back_kernel,
        grid=(pairs,),
        in_specs=[wide, narrow, narrow, narrow, fixed, fixed],
        out_specs=wide,
        out_shape=jax.ShapeDtypeStruct((LEN, pairs * PAIR), BF),
        compiler_params=params(56),
        cost_estimate=cost(5 * pairs),
    )(qkv, grad, mixed, log_total, cos, sin)


def mix_kernel(start, groups, count, last, *refs):
    mixed = refs[:count]
    wo, wt, ao, at = refs[count : count + 4]
    a = ao[...].astype(F32)
    b = at[...].astype(F32)
    for index in range(count):
        left = mixed[index][...]
        depth = left.shape[1]
        step, low = start + index // groups, index % groups * depth
        a = a + nn(left, wo[step, low : low + depth, :])
        b = b + nn(left, wt[step, low : low + depth, :])
    if not last:
        ro, rt = refs[count + 4 :]
    else:
        go, gt, ro, rt, no, nt_ = refs[count + 4 :]
        total = jnp.sum(a * a, axis=1, keepdims=True) + jnp.sum(b * b, axis=1, keepdims=True)
        scale = lax.rsqrt(total / (a.shape[1] + b.shape[1]) + norm_epsilon)
        no[...] = (a * scale * go[...]).astype(BF)
        nt_[...] = (b * scale * gt[...]).astype(BF)
    ro[...] = a
    rt[...] = b


def mix(mixed, wo, wt, ao, at, start, gains=None):
    depth, half = wo.shape[1:]
    count = len(mixed)
    groups = depth // mixed[0].shape[1]
    steps = count // groups
    rows = 256
    if start % steps == 0:
        weight = pl.BlockSpec((steps, depth, half), lambda i: (start // steps, 0, 0))
        offset = 0
    else:
        weight = pl.BlockSpec(wo.shape, lambda i: (0, 0, 0))
        offset = start
    left = pl.BlockSpec((rows, depth // groups), lambda i: (i, 0))
    part = pl.BlockSpec((rows, half), lambda i: (i, 0))
    gain = pl.BlockSpec((1, half), lambda i: (0, 0))
    last = gains is not None
    more = list(gains) if last else []
    return pl.pallas_call(
        functools.partial(mix_kernel, offset, groups, count, last),
        grid=(LEN // rows,),
        in_specs=[left] * count + [weight] * 2 + [part] * 2 + [gain] * len(more),
        out_specs=[part] * (4 if last else 2),
        out_shape=[jax.ShapeDtypeStruct((LEN, half), F32)] * 2
        + [jax.ShapeDtypeStruct((LEN, half), BF)] * (2 if last else 0),
        compiler_params=params(56),
        cost_estimate=cost(3 * count),
    )(*mixed, wo, wt, ao, at, *more)


def feed_kernel(no, nt_, back, gwo, gwt, uwo, uwt, hidden, gate_grad, upper_grad):
    gate = nn(no[...], gwo[...]) + nn(nt_[...], gwt[...])
    upper = nn(no[...], uwo[...]) + nn(nt_[...], uwt[...])
    sigmoid = 1.0 / (1.0 + jnp.exp(-gate))
    silu = gate * sigmoid
    hidden[...] = (silu * upper).astype(BF)
    hidden_grad = back[...]
    gate_grad[...] = (hidden_grad * upper * sigmoid * (1.0 + gate * (1.0 - sigmoid))).astype(BF)
    upper_grad[...] = (hidden_grad * silu).astype(BF)


def feed(no, nt_, back, gwo, gwt, uwo, uwt):
    half, units = gwo.shape
    tokens = pl.BlockSpec((LEN, half), lambda i: (0, 0))
    weight = pl.BlockSpec((half, BLOCK), lambda i: (0, i))
    out = pl.BlockSpec((LEN, BLOCK), lambda i: (0, i))
    return pl.pallas_call(
        feed_kernel,
        grid=(units // BLOCK,),
        in_specs=[tokens] * 2 + [out] + [weight] * 4,
        out_specs=[out] * 3,
        out_shape=[jax.ShapeDtypeStruct((LEN, units), BF)] * 3,
        compiler_params=params(60),
        cost_estimate=cost(26),
    )(no, nt_, back, gwo, gwt, uwo, uwt)


def product_kernel(kind, terms, more, *refs):
    lefts, rights = refs[:terms], refs[terms : 2 * terms]
    out = refs[2 * terms + more]
    if kind == "tn":
        turned = refs[2 * terms + more + 1 :]

        @pl.when(pl.program_id(0) == 0)
        def _():
            for left, kept in zip(lefts, turned):
                kept[...] = left[...].T

        lefts = turned
    dot = nt if kind == "nt" else nn
    total = refs[2 * terms][...].astype(F32) if more else None
    for left, right in zip(lefts, rights):
        term = dot(left[...], right[...])
        total = term if total is None else total + term
    out[...] = total.astype(out.dtype)


def product(kind, lefts, rights, kind_out=BF, extra=None, part=None, tile=512):
    which, parts = part or (0, 1)
    rows = lefts[0].shape[1 if kind == "tn" else 0]
    columns = rights[0].shape[0 if kind == "nt" else 1] // parts
    tile = min(tile, columns)
    first = which * (columns // tile)
    fixed = [pl.BlockSpec(v.shape, lambda i: (0, 0)) for v in lefts]
    if kind == "nt":
        moving = [pl.BlockSpec((tile, v.shape[1]), lambda i: (first + i, 0)) for v in rights]
    else:
        moving = [pl.BlockSpec((v.shape[0], tile), lambda i: (0, first + i)) for v in rights]
    out = pl.BlockSpec((rows, tile), lambda i: (0, i))
    more = [] if extra is None else [extra]
    return pl.pallas_call(
        functools.partial(product_kernel, kind, len(lefts), len(more)),
        grid=(columns // tile,),
        in_specs=fixed + moving + [out] * len(more),
        out_specs=out,
        out_shape=jax.ShapeDtypeStruct((rows, columns), kind_out),
        scratch_shapes=[pltpu.VMEM(v.shape[::-1], BF) for v in lefts] if kind == "tn" else [],
        compiler_params=params(60),
        cost_estimate=cost(1 + len(lefts) * lefts[0].size * columns / 3.4e8),
    )(*lefts, *rights, *more)


def beside_kernel(tiles, more, *refs):
    left, first, second = refs[:3]
    out, turned = refs[3 + more :]
    at = pl.program_id(0)

    @pl.when(at == 0)
    def _():
        turned[...] = left[...].T

    def store(right):
        total = nn(turned[...], right[...])
        if more:
            total = total + refs[3][...].astype(F32)
        out[...] = total.astype(out.dtype)

    @pl.when(at < tiles)
    def _():
        store(first)

    @pl.when(at >= tiles)
    def _():
        store(second)


def product_beside(left, first, second, extra=None, tile=512):
    depth, rows = left.shape
    columns = first.shape[1]
    tile = min(tile, columns)
    tiles = columns // tile
    out = pl.BlockSpec((rows, tile), lambda i: (0, i))
    more = [] if extra is None else [extra]
    return pl.pallas_call(
        functools.partial(beside_kernel, tiles, len(more)),
        grid=(2 * tiles,),
        in_specs=[
            pl.BlockSpec(left.shape, lambda i: (0, 0)),
            pl.BlockSpec((depth, tile), lambda i: (0, jnp.minimum(i, tiles - 1))),
            pl.BlockSpec((depth, tile), lambda i: (0, jnp.maximum(i - tiles, 0))),
        ]
        + [out] * len(more),
        out_specs=out,
        out_shape=jax.ShapeDtypeStruct((rows, 2 * columns), BF),
        scratch_shapes=[pltpu.VMEM((rows, depth), BF)],
        compiler_params=params(60),
        cost_estimate=cost(16),
    )(left, first, second, *more)


def swap_row(values):
    return lax.ppermute(values, "row", [(0, 1), (1, 0)])


class Ring:
    def __init__(self):
        count = lax.axis_size("col")
        self.count = count
        self.order = list(range(0, count, 2)) + list(range(count - 1, 0, -2))
        index = lax.axis_index("col")
        self.here = jnp.where(index % 2 == 0, index // 2, count - 1 - index // 2)
        self.core = lax.axis_index("row")

    def shift(self, values, by=1):
        count, order = self.count, self.order
        pairs = [(order[p], order[(p + by) % count]) for p in range(count)]
        return lax.ppermute(values, "col", pairs)

    def owner(self, back):
        count = self.count
        at = (self.here + (2 * count - back)) % count
        return jnp.where(at < count // 2, 2 * at, 2 * (count - 1 - at) + 1)

    def split(self, owner):
        per = self.count // 2
        return owner // per, owner % per

    def place(self, halves, direction):
        rows, columns = halves[0][0].shape
        whole = rows * len(halves)
        out = jnp.zeros((self.count * whole, columns), halves[0][0].dtype)
        for low, blocks in enumerate(halves):
            for step, block in enumerate(blocks):
                sequence, at = self.split(self.owner(direction * step))
                slot = jnp.where(sequence == self.core, 0, self.count // 2) + at
                out = lax.dynamic_update_slice(out, block, (slot * whole + low * rows, 0))
        return out

    def term(self, own, other, back):
        rows = own.shape[0] * 2 // self.count
        sequence, at = self.split(self.owner(back))
        take = lambda values: lax.dynamic_slice_in_dim(values, at * rows, rows, 0)
        return jnp.where(sequence == self.core, take(own), take(other))


def halve(values, bit, axis):
    size = values.shape[axis] // 2
    return lax.dynamic_slice_in_dim(values, bit * size, size, axis)


def join(values, others, bit, axis):
    first = jnp.where(bit == 0, values, others)
    second = jnp.where(bit == 0, others, values)
    return jnp.concatenate([first, second], axis=axis)


class Square:
    def __init__(self):
        index = lax.axis_index("dp")
        bits = (index % 2, index // 2)
        hops = tuple(
            lambda v, flip=flip: lax.ppermute(v, "dp", [(i, i ^ flip) for i in range(4)])
            for flip in (1, 2)
        )
        self.bits, self.hops = bits, hops
        self.index = index

    def send(self, parts, phase, axis):
        got = []
        for which, addends in enumerate(parts):
            turn = which ^ (phase - 1)
            out = sum(halve(v, 1 - self.bits[turn], axis).astype(F32) for v in addends)
            got.append(self.hops[turn](out.astype(BF)))
        return got

    def add(self, parts, got, phase, axis, kind=F32):
        kept = []
        for which, addends in enumerate(parts):
            turn = which ^ (phase - 1)
            out = sum(halve(v, self.bits[turn], axis).astype(F32) for v in addends)
            kept.append((out + got[which].astype(F32)).astype(kind))
        return kept

    def hop(self, parts, phase):
        return [self.hops[which ^ (phase - 1)](v) for which, v in enumerate(parts)]

    def join(self, parts, got, phase, axis):
        return [
            join(v, got[which], self.bits[which ^ (phase - 1)], axis)
            for which, v in enumerate(parts)
        ]


def row_total(values):
    return values + swap_row(values)


def shards(
    block_input,
    attn_gain,
    attn_weight,
    out_weight,
    feed_gain,
    gate_weight,
    up_weight,
    down_weight,
    out_cotangent,
):
    ring = Ring()
    square = Square()
    count, core = ring.count, ring.core
    rows, half = block_input.shape
    size = rows // 2
    width = 2 * half
    own_sequence, own_at = ring.split(lax.axis_index("col"))
    local = own_sequence == core

    steps = count - 1
    s = dict(
        x=block_input,
        cot=out_cotangent,
        aw=attn_weight,
        gw=gate_weight,
        uw=up_weight,
        dw=down_weight,
        gains=jnp.concatenate([attn_gain[None, :], feed_gain[None, :]], axis=0),
    )

    def tie(*held):
        kept = {name: s.pop(name) for name in held if name in s}
        fixed = lax.optimization_barrier(dict(s))
        s.clear()
        s.update(fixed)
        s.update(kept)

    def push(name):
        s[name] = s[name] + [ring.shift(s[name][-1])]

    def reduce_step(name, k):
        term = ring.term(s[name + "_own"], s[name + "_other"], k + 1)
        if k:
            term = (s[name].astype(F32) + term.astype(F32)).astype(BF)
        s[name] = ring.shift(term)

    def reduce_end(name):
        own, other = s.pop(name + "_own"), s.pop(name + "_other")
        return s.pop(name).astype(F32) + ring.term(own, other, count).astype(F32)

    quarter = out_weight.shape[0] // 4
    s["qs"] = [lax.dynamic_slice_in_dim(out_weight, square.index * quarter, quarter, 0)]
    s["xs"], s["cs"] = [s["x"]], [s["cot"]]
    for k in range(steps):
        push("xs")
        if k == 0:
            s["aw2"] = swap_row(s["aw"])
            s["gains2"] = swap_row(s["gains"])
            s["cos"], s["sin"] = rope_tables()
            inputs = s["x"].astype(F32)
            squares = jnp.sum(inputs * inputs, axis=1)
            s["first_scale"] = lax.rsqrt(row_total(squares) / width + norm_epsilon)
        if k == 1:
            s["gw2"] = swap_row(s["gw"])
        if k == 2:
            s["uw2"] = swap_row(s["uw"])
        if k >= 2 and len(s["qs"]) < count:
            push("qs")
        tie()

    push("cs")
    if len(s["qs"]) < count:
        push("qs")
    both = ring.place([s.pop("xs")], 1)
    s["xo"] = both[:LEN]
    s["xt"] = swap_row(both[LEN:])
    s["n1o"], s["n1t"], s["qkv"], s["scale1"] = project(
        s["xo"],
        s["xt"],
        s["gains"][:1],
        s["gains2"][:1],
        s["aw"],
        s["aw2"],
        s["cos"],
        s["sin"],
    )
    tie()
    for k in range(1, steps - 1):
        push("cs")
        if len(s["qs"]) < count:
            push("qs")
        if k == 1:
            mixed, s["log_total"] = attend(s["qkv"], 0, 1)
            s["mixed"] = [mixed]
        tie()

    push("mixed")
    push("cs")
    s["dw2"] = swap_row(s["dw"])
    held = jnp.stack(s.pop("qs"), axis=0)
    s["ow"] = [held[: count // 2], held[count // 2 :]]
    s["ow_got"] = square.hop(s["ow"], 1)
    tie()
    push("mixed")
    s["ow"] = square.join(s["ow"], s.pop("ow_got"), 1, 1)
    s["ow_got"] = square.hop(s["ow"], 2)
    both = ring.place([s.pop("cs")], 1)
    s["co"] = both[:LEN]
    s["ct"] = swap_row(both[LEN:])
    s["back"] = product("nt", [s["co"]], [s["dw"]], F32)
    s["back"] = product("nt", [s["ct"]], [s["dw2"]], F32, s["back"])
    tie()
    for k in range(2, steps):
        push("mixed")
        if k == 2:
            first, second = square.join(s.pop("ow"), s.pop("ow_got"), 2, 1)
            shape = second.shape
            second = second.reshape(shape[0], 2, 2, quarter, half).swapaxes(1, 2).reshape(shape)
            s["owo"] = jnp.concatenate([first, second], axis=0)
            s["owt"] = swap_row(s["owo"])
            s["ro"], s["rt"] = mix(s["mixed"][:3], s["owo"], s["owt"], s["xo"], s["xt"], 0)
        tie()

    gains, gains2 = s["gains"], s["gains2"]
    s["ro"], s["rt"], s["n2o"], s["n2t"] = mix(
        s["mixed"][3:], s["owo"], s["owt"], s["ro"], s["rt"], 3, (gains[1:], gains2[1:])
    )
    s["hidden"], s["gg"], s["ug"] = feed(
        s["n2o"], s["n2t"], s.pop("back"), s["gw"], s["gw2"], s["uw"], s["uw2"]
    )
    tie()
    s["dn_other"] = product("nn", [s["hidden"]], [s.pop("dw2")])
    tie()
    s["dn_other"] = swap_row(s["dn_other"])
    s["dn_own"] = product("nn", [s["hidden"]], [s.pop("dw")])
    tie()
    reduce_step("dn", 0)
    s["down_other"] = product("tn", [s["hidden"]], [s.pop("ct")])
    tie("dn")
    s["down_other"] = swap_row(s["down_other"])
    s["sg_other"] = product("nt", [s["gg"], s["ug"]], [s.pop("gw2"), s.pop("uw2")])
    tie()
    s["sg_other"] = swap_row(s["sg_other"])
    s["down"] = product("tn", [s.pop("hidden")], [s.pop("co")], extra=s.pop("down_other"))
    tie()
    s["down"] = lax.psum_scatter(s["down"], "dp", scatter_dimension=0, tiled=True)
    s["sg_own"] = product("nt", [s["gg"], s["ug"]], [s.pop("gw"), s.pop("uw")])
    tie("down")

    take = lambda v: lax.dynamic_slice_in_dim(v, own_at * rows, rows, 0)
    reduce_step("sg", 0)
    s["both_other"] = product_beside(s.pop("n2t"), s["gg"], s["ug"])
    s["res"] = jnp.where(local, take(s.pop("ro")), swap_row(take(s.pop("rt"))))
    tie()
    s["down"] = lax.all_gather(s["down"], "dp", axis=0, tiled=True)
    reduce_step("sg", 1)
    s["both_other"] = swap_row(s["both_other"])
    residual = s["res"]
    squares = row_total(jnp.sum(residual * residual, axis=1))
    s["second_scale"] = lax.rsqrt(squares / width + norm_epsilon)

    def tokens(which):
        part = [
            lax.dynamic_slice_in_dim(v, own_at * rows + which * size, size, 0)
            for v in s["mixed"]
        ]
        return jnp.concatenate(
            [v[:, q * quarter : (q + 1) * quarter] for q in range(4) for v in part], axis=1
        )

    s["mixed_rows"] = jnp.where(local, tokens(core), swap_row(tokens(1 - core)))
    s["mixed"] = s["mixed"][0]
    s["both"] = product_beside(s.pop("n2o"), s.pop("gg"), s.pop("ug"), s.pop("both_other"))
    tie("down")
    for k in range(2, steps):
        reduce_step("sg", k)
        if k == 2:
            s["both"] = lax.psum_scatter(s["both"], "dp", scatter_dimension=0, tiled=True)
        tie("both", "down")

    reduce_step("dn", 1)
    second_grad = reduce_end("sg")
    second_hat = s["res"] * s["second_scale"][:, None]
    s["feed_part"] = jnp.sum(second_grad * second_hat, axis=0, keepdims=True)
    weighted = second_grad * s["gains"][1:]
    second_mean = row_total(jnp.sum(weighted * second_hat, axis=1)) / width
    s["residual_grad"] = s["cot"].astype(F32) + s["second_scale"][:, None] * (
        weighted - second_hat * second_mean[:, None]
    )
    low = s["residual_grad"].astype(BF)
    s["low_own"] = lax.dynamic_slice_in_dim(low, core * size, size, 0)
    s["low_other"] = swap_row(lax.dynamic_slice_in_dim(low, (1 - core) * size, size, 0))
    heads = s["mixed"].shape[1]
    grads = product(
        "nt",
        [s["low_own"], s["low_other"]],
        [s.pop("owo").reshape(-1, half), s.pop("owt").reshape(-1, half)],
    )
    s["grads"] = [grads[:, i * heads : (i + 1) * heads] for i in range(count)]
    tie("both")

    s["grads"] = [ring.shift(v, -i) if i else v for i, v in enumerate(s["grads"])]
    other = swap_row(product("tn", [s["mixed_rows"]], [s.pop("low_other")]))
    s["out"] = product("tn", [s.pop("mixed_rows")], [s.pop("low_own")], extra=other)
    tie("both")

    for k in range(2, steps):
        reduce_step("dn", k)
        if k < steps - 1:
            tie("both", "down")
    s["out"] = lax.psum_scatter(s["out"], "dp", scatter_dimension=0, tiled=True)
    both = ring.place([s.pop("grads")], -1)
    mine, theirs = both[: LEN // 2], swap_row(both[LEN // 2 :])
    mine, theirs = (v.reshape(-1, size, heads) for v in (mine, theirs))
    grad = jnp.stack(
        [jnp.where(core == 0, mine, theirs), jnp.where(core == 0, theirs, mine)], axis=1
    ).reshape(LEN, heads)
    s["pg"] = attend_back(
        s.pop("qkv"), grad, s.pop("mixed"), s.pop("log_total"), s.pop("cos"), s.pop("sin")
    )
    tie("out")
    s["both"] = lax.all_gather(s["both"], "dp", axis=0, tiled=True)
    s["fg_local"] = product("nt", [s["pg"]], [s.pop("aw2")])
    s["attn_other"] = product("tn", [s.pop("n1t")], [s["pg"]], tile=PAIR)
    tie("both", "out")
    s["fg_other"] = swap_row(s["fg_local"])
    s["attn_other"] = swap_row(s["attn_other"])
    s["fg_own"] = product("nt", [s["pg"]], [s.pop("aw")])
    tie("both", "out")

    def split(name):
        values = s[name]
        cut = values.shape[0] // 2
        s[name] = [[values[:cut]], [values[cut:]]]
        s[name + "_got"] = square.send(s[name], 1, 0)

    def phase(name, which):
        got = s.pop(name + "_got")
        if which == 2:
            s[name] = [[v] for v in square.add(s[name], got, 1, 0)]
            s[name + "_got"] = square.send(s[name], 2, 0)
        if which == 3:
            s[name] = square.add(s[name], got, 2, 0, BF)
            s[name + "_got"] = square.hop(s[name], 2)
        if which == 4:
            s[name] = square.join(s[name], got, 2, 0)
            s[name + "_got"] = square.hop(s[name], 1)
        if which == 5:
            halves = square.join(s[name], got, 1, 0)
            s[name] = jnp.concatenate(halves, axis=0).astype(F32)

    def out_step(k):
        term = s["out"][(k + 1) % count]
        if k:
            term = (s["out_ring"].astype(F32) + term.astype(F32)).astype(BF)
        s["out_ring"] = ring.shift(term)

    reduce_step("fg", 0)
    s["attn"] = product("tn", [s.pop("n1o")], [s.pop("pg")], extra=s.pop("attn_other"), tile=PAIR)
    scale1 = s.pop("scale1")[:, :1]
    part = lambda grad, inputs: jnp.sum(
        grad.astype(F32) * (inputs.astype(F32) * scale1), axis=0, keepdims=True
    )
    other = swap_row(part(s.pop("fg_local"), s.pop("xt")))
    s["parts"] = jnp.concatenate(
        [part(s["fg_own"], s.pop("xo")) + other, s.pop("feed_part")], axis=0
    )
    tie("both")
    reduce_step("fg", 1)
    split("attn")
    s["parts"] = s["parts"] + square.hops[0](s["parts"])
    s["output"] = (s.pop("res") + reduce_end("dn")).astype(BF)
    s["down"] = s["down"].astype(F32)
    tie("both")
    s["out"] = s["out"].reshape(count, quarter, half)
    for k in range(2, steps):
        reduce_step("fg", k)
        if k == 2:
            phase("attn", 2)
            out_step(0)
            s["parts"] = s["parts"] + square.hops[1](s["parts"])
            tie("both", "fg")
            phase("attn", 3)
            out_step(1)
            parts = s.pop("parts")
            s["parts"] = sum([ring.shift(parts, i) for i in range(1, count)], parts)
        tie("both")
    phase("attn", 4)
    for k in range(2, steps):
        out_step(k)
    first_grad = reduce_end("fg")
    scale = s["first_scale"][:, None]
    first_hat = s["x"].astype(F32) * scale
    weighted = first_grad * s["gains"][:1]
    first_mean = row_total(jnp.sum(weighted * first_hat, axis=1)) / width
    s["input"] = s["residual_grad"] + scale * (weighted - first_hat * first_mean[:, None])
    tie("both")
    out = (s.pop("out_ring").astype(F32) + s["out"][0].astype(F32)).astype(BF)
    s["out"] = join(out, square.hops[0](out), square.bits[0], 0)
    tie()
    s["out"] = join(s["out"], square.hops[1](s["out"]), square.bits[1], 0).astype(F32)
    phase("attn", 5)
    units = gate_weight.shape[1]
    s["gate"] = s["both"][:, :units].astype(F32)
    s["up"] = s.pop("both")[:, units:].astype(F32)
    return (
        s["output"],
        s["input"],
        s["parts"][0],
        s["attn"],
        s["out"],
        s["parts"][1],
        s["gate"],
        s["up"],
        s["down"],
    )


def solution(mesh):
    in_specs = (
        P(("dp", "col"), "row"),
        P("row"),
        P("row", "col"),
        P("col", "row"),
        P("row"),
        P("row", "col"),
        P("row", "col"),
        P("col", "row"),
        P(("dp", "col"), "row"),
    )
    out_specs = (
        P(("dp", "col"), "row"),
        P(("dp", "col"), "row"),
        P("row"),
        P("row", "col"),
        P("col", "row"),
        P("row"),
        P("row", "col"),
        P("row", "col"),
        P("col", "row"),
    )
    return jax.shard_map(shards, mesh=mesh, in_specs=in_specs, out_specs=out_specs, check_vma=False)
```
